1024 devices in a mesh: emb: 64 (over z, y), bal: 8 (over x), rep: 2 (over core).
Axes of the slice: x: 8, y: 8, z: 8, core: 2. Of those that a mesh axis runs over, the one named last changes fastest.
Arguments:
- table: bfloat16 [16384, 512], P('emb'), may hold values from -4 to 4
- served_rows: int32 [64, 8, 2, 512], P('emb', 'bal', 'rep'), may hold values from 0 to 255
- w_in: bfloat16 [512, 2048], replicated, may hold values from -0.25 to 0.25
- w_out: bfloat16 [512, 512], replicated, may hold values from -0.25 to 0.25
- lookup_slots: int32 [128, 1024, 2], P(('emb', 'rep'), 'bal'), may hold values from 0 to 511, as said below
- block_users: int32 [128, 8], P(('emb', 'rep')), may hold values from 0 to 1, as said below
- out_grad: bfloat16 [128, 1024, 512], P(('emb', 'rep'), 'bal'), may hold values from -6 to 6
Outputs:
- layer_out: bfloat16 [128, 1024, 512], P(('emb', 'rep'), 'bal')
- table_grad: float32 [16384, 512], P('emb')
The draws below stay inside these ranges and needn't reach their ends.
Inputs may be any that keep to these rules, and one draw needn't show every extreme that they name: `lookup_slots`: on one device (one group g and one b), the 2 entries of all its 128 events are distinct, each naming shard p // 8 and slot p % 8. `block_users`: never falling along a group; every user 0 to 1 of every group holds 2 to 6 blocks, and in every draw some group has a user with exactly 6 blocks.
All inputs are finite; a program needn't handle non-finite values.
Results may differ from the reference program's by a relative error of at most 0.02.
Values may be sent and summed in bfloat16 or wider, within the bound.
A program may use at most 64 MiB of HBM per device.

```python
import jax
import jax.numpy as jnp
from jax import lax

D = 512
HEADS = 4
FEATS = 2
BLK = 128
USERS = 2
TOK_DEV = 128
TROWS = 256
CAP = 8
GROUP_TOK = 1024
GROUP_BLK = 8
MIN_BLK = 2
GROUPS = 128
TABLE_ROWS = 16384
N_EMB = 64
N_BAL = 8
N_REP = 2


def draw_lookup_slots(key, part):
    key = jax.random.fold_in(key, 7)
    device_keys = jax.random.split(key, GROUPS * N_BAL)

    def one_device(device_key):
        return jax.random.permutation(device_key, N_EMB * CAP)[:TOK_DEV * FEATS].astype(jnp.int32)
    picked = jax.vmap(one_device)(device_keys)
    return picked.reshape(GROUPS, GROUP_TOK, FEATS)


def draw_block_users(key, part):
    key = jax.random.fold_in(key, 11)
    spare_blocks = GROUP_BLK - USERS * MIN_BLK
    slot_count = spare_blocks + USERS - 1
    group_keys = jax.random.split(key, GROUPS)
    forced_group = jax.random.randint(jax.random.fold_in(key, 5), (), 0, GROUPS)
    forced_user = jax.random.randint(jax.random.fold_in(key, 6), (), 0, USERS)
    user_ids = jnp.arange(USERS, dtype=jnp.int32)
    block_ids = jnp.arange(GROUP_BLK, dtype=jnp.int32)

    def one_group(group_key, group_id):
        shuffled = jax.random.permutation(group_key, slot_count).astype(jnp.int32)
        bar_mark = (shuffled < USERS - 1).astype(jnp.int32)
        segment = jnp.cumsum(bar_mark)
        star_hits = (segment[:, None] == user_ids[None, :]) & (bar_mark[:, None] == 0)
        extras = jnp.sum(star_hits.astype(jnp.int32), axis=0)
        forced_extras = jnp.where(user_ids == forced_user, spare_blocks, 0).astype(jnp.int32)
        counts = MIN_BLK + jnp.where(group_id == forced_group, forced_extras, extras)
        block_ends = jnp.cumsum(counts)
        passed = block_ids[:, None] >= block_ends[None, :USERS - 1]
        return jnp.sum(passed.astype(jnp.int32), axis=1).astype(jnp.int32)
    return jax.vmap(one_group)(group_keys, jnp.arange(GROUPS, dtype=jnp.int32))


def touch_ends(array, stream_key, low, high):
    longest = array.shape.index(max(array.shape))
    spots = []
    for shift in (0, 1):
        where = [jax.random.randint(jax.random.fold_in(stream_key, axis), (), 0, length) for axis, length in enumerate(array.shape)]
        where[longest] = (where[longest] + shift) % array.shape[longest]
        spots.append(tuple(where))
    return array.at[spots[0]].set(low).at[spots[1]].set(high)


def levels(stream_key, dims, cuts, least, high):
    factor_of = 1.0
    for dim, blocks in cuts:
        steps = jax.random.uniform(jax.random.fold_in(jax.random.fold_in(stream_key, 6), dim), (blocks,), jnp.float32, least / len(cuts), high / len(cuts))
        factor_of = factor_of * jnp.repeat(jnp.exp(steps), dims[dim] // blocks).reshape((-1,) + (1,) * (len(dims) - 1 - dim))
    return factor_of


def centred(own_key, shape, width, most, shards=(), kind=jnp.bfloat16):
    level = levels(own_key, shape, shards, -0.22, 0.18) if shards else 1.0
    entries = jax.random.normal(own_key, shape, jnp.float32) * width * level
    return jnp.minimum(jnp.maximum(entries, -most), most).astype(kind)


def setup_inputs(seed: int = 0) -> dict:
    streams_of = jax.random.split(jax.random.key(seed), 8)
    return {
        "table": centred(streams_of[0], (TABLE_ROWS, D), 0.7, 4.0, ((0, 64),)),
        "served_rows": touch_ends(jax.random.randint(streams_of[1], (N_EMB, N_BAL, N_REP, N_EMB * CAP), 0, TROWS), jax.random.fold_in(streams_of[1], 1), 0, TROWS - 1).astype(jnp.int32),
        "w_in": centred(streams_of[2], (D, 4 * D), D ** -0.5, 0.25),
        "w_out": centred(streams_of[3], (D, D), D ** -0.5, 0.25),
        "lookup_slots": draw_lookup_slots(jax.random.fold_in(streams_of[7], 71), 0),
        "block_users": draw_block_users(jax.random.fold_in(streams_of[7], 71), 0),
        "out_grad": centred(streams_of[6], (GROUPS, GROUP_TOK, D), 1.0, 6.0, ((0, 128), (1, 8))),
    }


epsilon = 1e-05

def normalize(inputs):
    average = lax.optimization_barrier(jnp.mean(inputs, axis=-1, keepdims=True))
    centered = inputs - average
    spread = jnp.sqrt(lax.optimization_barrier(jnp.mean(centered * centered, axis=-1, keepdims=True)) + epsilon)
    return (centered / spread, spread)

def normalize_back(grads, normed, spread):
    first_term = lax.optimization_barrier(jnp.mean(grads, axis=-1, keepdims=True))
    second_term = lax.optimization_barrier(jnp.mean(grads * normed, axis=-1, keepdims=True))
    return (grads - first_term - normed * second_term) / spread

def silu_slope(inputs):
    sigmoid_val = jax.nn.sigmoid(inputs)
    return sigmoid_val * (1.0 + inputs * (1.0 - sigmoid_val))

def reference(table, served_rows, w_in, w_out, lookup_slots, block_users, out_grad):
    head_dim = D // HEADS
    inv_root = 1.0 / head_dim ** 0.5
    token_pos = jnp.arange(GROUP_TOK, dtype=jnp.int32)
    bal_of = (token_pos // TOK_DEV).astype(jnp.int32)

    def one_group(grad_total, inputs):
        group_id, lookup_pos, users, grad_rows = inputs
        emb_id = group_id // N_REP
        rep_id = group_id % N_REP
        shard_id = lookup_pos // CAP
        slot_id = lookup_pos % CAP
        local_row = served_rows[shard_id, bal_of[:, None], rep_id, emb_id * CAP + slot_id]
        global_row = (shard_id * TROWS + local_row).astype(jnp.int32)
        events = lax.optimization_barrier(jnp.sum(table[global_row].astype(jnp.float32), axis=1))
        normed_in, sigma_in = normalize(events)
        pre_act = jnp.dot(normed_in.astype(jnp.bfloat16), w_in, preferred_element_type=jnp.float32)
        activations = jax.nn.silu(pre_act).astype(jnp.bfloat16)
        gate_part = activations[:, :D].astype(jnp.float32)
        value_heads = activations[:, D:2 * D].astype(jnp.float32).reshape(GROUP_TOK, HEADS, head_dim)
        query_heads = activations[:, 2 * D:3 * D].astype(jnp.float32).reshape(GROUP_TOK, HEADS, head_dim)
        key_heads = activations[:, 3 * D:].astype(jnp.float32).reshape(GROUP_TOK, HEADS, head_dim)
        user_tok = jnp.repeat(users, BLK, total_repeat_length=GROUP_TOK)
        same_user = user_tok[:, None] == user_tok[None, :]
        user_length = lax.optimization_barrier(jnp.sum(same_user.astype(jnp.float32), axis=1))
        visible = same_user & (token_pos[:, None] >= token_pos[None, :])
        scores = jnp.einsum('ihd,jhd->hij', query_heads, key_heads) * inv_root
        weights = jnp.where(visible[None], jax.nn.silu(scores) / user_length[None, :, None], 0.0).astype(jnp.bfloat16)
        weights_f = weights.astype(jnp.float32)
        attended = jnp.einsum('hij,jhd->ihd', weights_f, value_heads).reshape(GROUP_TOK, D)
        normed_att, sigma_att = normalize(attended)
        mixed = (normed_att * gate_part).astype(jnp.bfloat16)
        layer_out = (events + jnp.dot(mixed, w_out, preferred_element_type=jnp.float32)).astype(jnp.bfloat16)
        d_mixed = jnp.dot(grad_rows, w_out.T, preferred_element_type=jnp.float32)
        d_gate = d_mixed * normed_att
        d_att = normalize_back(d_mixed * gate_part, normed_att, sigma_att).astype(jnp.bfloat16)
        d_heads = d_att.astype(jnp.float32).reshape(GROUP_TOK, HEADS, head_dim)
        d_weights = jnp.einsum('ihd,jhd->hij', d_heads, value_heads)
        d_scores = jnp.where(visible[None], d_weights * silu_slope(scores) / user_length[None, :, None], 0.0).astype(jnp.bfloat16)
        d_scores_f = d_scores.astype(jnp.float32)
        d_values = jnp.einsum('hij,ihd->jhd', weights_f, d_heads).reshape(GROUP_TOK, D)
        d_keys = jnp.einsum('hij,ihd->jhd', d_scores_f, query_heads).reshape(GROUP_TOK, D) * inv_root
        d_queries = jnp.einsum('hij,jhd->ihd', d_scores_f, key_heads).reshape(GROUP_TOK, D) * inv_root
        d_acts = jnp.concatenate([d_gate, d_values, d_queries, d_keys], axis=1)
        d_pre = (d_acts * silu_slope(pre_act)).astype(jnp.bfloat16)
        d_normed = jnp.dot(d_pre, w_in.T, preferred_element_type=jnp.float32)
        d_events = (grad_rows.astype(jnp.float32) + normalize_back(d_normed, normed_in, sigma_in)).astype(jnp.bfloat16)
        spread_rows = jnp.broadcast_to(d_events.astype(jnp.float32)[:, None, :], (GROUP_TOK, FEATS, D)).reshape(GROUP_TOK * FEATS, D)
        grad_total = grad_total.at[global_row.reshape(-1)].add(spread_rows)
        return (grad_total, layer_out)
    start_grad = jnp.zeros((N_EMB * TROWS, D), jnp.float32)
    group_ids = jnp.arange(GROUPS, dtype=jnp.int32)
    table_grad, layer_out = lax.scan(one_group, start_grad, (group_ids, lookup_slots, block_users, out_grad))
    return (layer_out, table_grad)
```

```python
import functools
import math

import jax
import jax.numpy as jnp
from jax import lax
from jax.experimental import pallas as pl
from jax.experimental.pallas import tpu as pltpu
from jax.sharding import PartitionSpec as P

HEADS = 4
EPS = 1e-05
MESH = pl.DeviceIdType.MESH
F32 = jnp.float32
BF16 = jnp.bfloat16


def dot(a, b):
    return jnp.dot(a, b, preferred_element_type=F32)


def dot_nt(a, b):
    return lax.dot_general(a, b, (((1,), (1,)), ((), ())), preferred_element_type=F32)


def dot_tn(a, b):
    return lax.dot_general(a, b, (((0,), (0,)), ((), ())), preferred_element_type=F32)


def sigmoid(v):
    return 0.5 * jnp.tanh(0.5 * v) + 0.5


def silu(v):
    return v * sigmoid(v)


def silu_and_slope(v):
    s = sigmoid(v)
    y = v * s
    return y, s + y * (1.0 - s)


def row_mean(v):
    return jnp.mean(v, axis=-1, keepdims=True)


def layer_kernel(
    sizes,
    table_ref, idx_ref, lookup_ref, users_ref, w_in_hbm, w_out_hbm, grad_hbm,
    layer_ref, tgrad_ref,
    w_in, w_out, grad, zout, zin, zback, zret, onehot, look,
    events, normed, inv_in, act, slope, nrm, datt, kv, qall,
    wt, gt, gq, att, dq, dk, dv, gsend, rsbuf, agbuf,
    load_sem, a1_send, a1_recv, x1_send, x1_recv, x2_send, x2_recv,
    a2_send, a2_recv, rs_send, rs_recv, ag_send, ag_recv,
):
    n_emb, n_bal, n_rep = sizes
    tok, width = grad.shape
    half = width // 2
    slab = zout.shape[0] // n_emb
    cap = slab // 2
    trows = table_ref.shape[0]
    hd = width // HEADS
    inv_root = 1.0 / math.sqrt(hd)
    e = lax.axis_index("emb")
    b = lax.axis_index("bal")
    rep = lax.axis_index("rep")
    n_red = n_bal * n_rep
    mine = b * n_rep + rep
    part = gsend.shape[0] // n_red

    def red_peer(k):
        c = lax.rem(mine + k, n_red)
        return c, {"bal": lax.div(c, n_rep), "rep": lax.rem(c, n_rep)}

    loads = [
        pltpu.make_async_copy(src, dst, load_sem.at[i])
        for i, (src, dst) in enumerate(((w_in_hbm, w_in), (w_out_hbm, w_out), (grad_hbm, grad)))
    ]
    for load in loads:
        load.start()

    barrier = pltpu.get_barrier_semaphore()

    @pl.loop(1, n_emb)
    def _(k):
        pl.semaphore_signal(
            barrier, inc=1, device_id={"emb": lax.rem(e + k, n_emb)}, device_id_type=MESH
        )

    @pl.loop(1, n_red)
    def _(k):
        _, where = red_peer(k)
        pl.semaphore_signal(barrier, inc=1, device_id=where, device_id_type=MESH)

    rows_of = lax.broadcasted_iota(jnp.int32, onehot.shape, 0)
    onehot[...] = jnp.where(rows_of == idx_ref[...], 1.0, 0.0).astype(BF16)
    stacked = jnp.concatenate([table_ref[:, :half], table_ref[:, half:]], axis=0)
    zout[...] = dot_tn(onehot[...], stacked).astype(BF16)

    pl.semaphore_wait(barrier, n_emb - 1 + n_red - 1)

    def exchange(src, dst, send, recv):
        own = pl.ds(pl.multiple_of(e * slab, slab), slab)

        @pl.loop(1, n_emb)
        def _(k):
            to = lax.rem(e + k, n_emb)
            pltpu.make_async_remote_copy(
                src_ref=src.at[pl.ds(pl.multiple_of(to * slab, slab), slab)],
                dst_ref=dst.at[own],
                send_sem=send,
                recv_sem=recv,
                device_id={"emb": to},
                device_id_type=MESH,
            ).start()

        dst[own, :] = src[own, :]
        many = pl.ds(0, (n_emb - 1) * slab)
        return pltpu.make_async_remote_copy(
            src_ref=src.at[many],
            dst_ref=dst.at[many],
            send_sem=send,
            recv_sem=recv,
            device_id={"emb": lax.rem(e + 1, n_emb)},
            device_id_type=MESH,
        )

    first = exchange(zout, zin, a1_send, a1_recv)

    p = lookup_ref[...]
    slot = lax.shift_right_logical(p, int(math.log2(cap))) * slab + (p & (cap - 1))
    cols_of = lax.broadcasted_iota(jnp.int32, (tok, zout.shape[0]), 1)
    for h in range(2):
        q = slot + h * cap
        hit = (cols_of == q[:, 0:1]) | (cols_of == q[:, 1:2])
        look[h * tok : (h + 1) * tok, :] = jnp.where(hit, 1.0, 0.0).astype(BF16)

    my_user = users_ref[0, b]
    count = jnp.int32(0)
    for k in range(n_bal):
        count = count + jnp.where(users_ref[0, k] == my_user, 1, 0)
    inv_len = jnp.float32(0.0)
    for k in range(1, n_bal + 1):
        inv_len = jnp.where(count == k, jnp.float32(1.0 / (k * tok)), inv_len)

    for load in loads:
        load.wait()
    d_mixed = dot_nt(grad[...], w_out[...])

    first.wait_recv()
    two = dot(look[...], zin[...])
    events[...] = jnp.concatenate([two[:tok], two[tok:]], axis=1)
    ev = events[...]
    centered = ev - row_mean(ev)
    inv = lax.rsqrt(row_mean(centered * centered) + EPS)
    inv_in[...] = jnp.broadcast_to(inv, inv_in.shape)
    normed[...] = centered * inv
    nrm[0] = normed[...].astype(BF16)

    rows = tok // 2
    steps = n_bal // 2
    right = lax.rem(b + 1, n_bal)
    left = lax.rem(b + n_bal - 1, n_bal)

    def hop(buf, send, recv, way, step, c):
        if way == 0:
            src, dst, to = lax.rem(n_bal - step, n_bal), n_bal - 1 - step, right
        else:
            src, dst, to = step, step + 1, left
        piece = pl.ds(c * rows, rows)
        return pltpu.make_async_remote_copy(
            src_ref=buf.at[src, piece],
            dst_ref=buf.at[dst, piece],
            send_sem=send.at[way, step, c],
            recv_sem=recv.at[way, step, c],
            device_id={"bal": to},
            device_id_type=MESH,
        )

    lanes = [(way, c) for c in range(2) for way in range(2)]

    def ring_start(buf, send, recv):
        for way, c in lanes:
            if steps > 1 or way == c:
                hop(buf, send, recv, way, 0, c).start()

    def ring_rest(buf, send, recv, on_block):
        @pl.loop(0, steps)
        def _(step):
            for way, c in lanes:
                last = steps - 1 if way == c else steps - 2

                @pl.when(step <= last)
                def _():
                    hop(buf, send, recv, way, step, c).wait_recv()

                @pl.when(step + 1 <= last)
                def _():
                    hop(buf, send, recv, way, step + 1, c).start()

            @pl.loop(0, 2)
            def _(k):
                @pl.when((k == 0) | (step < steps - 1))
                def _():
                    on_block(jnp.where(k == 0, n_bal - 1 - step, step + 1))

    def ring_drain(buf, send, recv):
        @pl.loop(0, steps)
        def _(step):
            for way, c in lanes:
                last = steps - 1 if way == c else steps - 2

                @pl.when(step <= last)
                def _():
                    hop(buf, send, recv, way, step, c).wait_send()

    ring_start(nrm, x1_send, x1_recv)

    for k in (1, 2, 3, 0):
        cols = slice(k * width, (k + 1) * width)
        a, s = silu_and_slope(dot(nrm[0], w_in[:, cols]))
        act[:, cols] = a.astype(BF16)
        slope[:, cols] = s
    v_at, q_at, k_at = width, 2 * width, 3 * width

    def head(h, base=0):
        return slice(base + h * hd, base + (h + 1) * hd)

    tri_row = lax.broadcasted_iota(jnp.int32, (tok, tok), 0)
    tri_col = lax.broadcasted_iota(jnp.int32, (tok, tok), 1)
    for h in range(HEADS):
        q, k, v = act[:, head(h, q_at)], act[:, head(h, k_at)], act[:, head(h, v_at)]
        y, g = silu_and_slope(dot_nt(q, k) * inv_root)
        keep = tri_row >= tri_col
        att[:, head(h)] = dot(jnp.where(keep, y * inv_len, 0.0).astype(BF16), v)
        gq[0, h] = jnp.where(keep, g * inv_len, 0.0)
        y, g = silu_and_slope(dot_nt(k, q) * inv_root)
        keep = tri_row <= tri_col
        wt[0, h] = jnp.where(keep, y * inv_len, 0.0).astype(BF16)
        gt[0, h] = jnp.where(keep, g * inv_len, 0.0)

    def seen(j):
        return jnp.where(users_ref[0, j] == my_user, inv_len, jnp.float32(0.0))

    def forward_block(r):
        j = lax.rem(b + r, n_bal)
        f = seen(j)

        @pl.when(j < b)
        def _():
            x = nrm[r]
            kv[r, :, :width] = silu(dot(x, w_in[:, v_at : v_at + width])).astype(BF16)
            kv[r, :, width:] = silu(dot(x, w_in[:, k_at : k_at + width])).astype(BF16)
            for h in range(HEADS):
                k = kv[r, :, head(h, width)]
                y, g = silu_and_slope(dot_nt(act[:, head(h, q_at)], k) * inv_root)
                gq[r, h] = g * f
                att[:, head(h)] += dot((y * f).astype(BF16), kv[r, :, head(h)])

        @pl.when(j > b)
        def _():
            qall[r] = silu(dot(nrm[r], w_in[:, q_at : q_at + width])).astype(BF16)
            for h in range(HEADS):
                y, g = silu_and_slope(
                    dot_nt(act[:, head(h, k_at)], qall[r, :, head(h)]) * inv_root
                )
                gt[r, h] = g * f
                wt[r, h] = (y * f).astype(BF16)

    ring_rest(nrm, x1_send, x1_recv, forward_block)

    at = att[...]
    centered = at - row_mean(at)
    inv_att = lax.rsqrt(row_mean(centered * centered) + EPS)
    normed_att = centered * inv_att
    gate = act[:, :width].astype(F32)
    d_gated = d_mixed * gate
    d_att = (
        (d_gated - row_mean(d_gated) - normed_att * row_mean(d_gated * normed_att)) * inv_att
    ).astype(BF16)
    datt[0] = d_att
    ring_start(datt, x2_send, x2_recv)

    mixed = (normed_att * gate).astype(BF16)
    layer_ref[...] = (events[...] + dot(mixed, w_out[...])).astype(BF16)
    d_pre = (d_mixed * normed_att * slope[:, :width]).astype(BF16)
    gate_part = dot_nt(d_pre, w_in[:, :width])
    for h in range(HEADS):
        q, k, v = act[:, head(h, q_at)], act[:, head(h, k_at)], act[:, head(h, v_at)]
        d = datt[0, :, head(h)]
        ds = (dot_nt(d, v) * gq[0, h]).astype(BF16)
        dq[:, head(h)] = dot(ds, k)
        dv[:, head(h)] = dot(wt[0, h], d)
        dst = (dot_nt(v, d) * gt[0, h]).astype(BF16)
        dk[:, head(h)] = dot(dst, q)

    def backward_block(r):
        j = lax.rem(b + r, n_bal)

        @pl.when(j < b)
        def _():
            for h in range(HEADS):
                ds = (dot_nt(datt[0, :, head(h)], kv[r, :, head(h)]) * gq[r, h]).astype(BF16)
                dq[:, head(h)] += dot(ds, kv[r, :, head(h, width)])

        @pl.when(j > b)
        def _():
            for h in range(HEADS):
                d = datt[r, :, head(h)]
                dv[:, head(h)] += dot(wt[r, h], d)
                dst = (dot_nt(act[:, head(h, v_at)], d) * gt[r, h]).astype(BF16)
                dk[:, head(h)] += dot(dst, qall[r, :, head(h)])

    ring_rest(datt, x2_send, x2_recv, backward_block)

    d_normed = gate_part
    for base, acc, scale in ((v_at, dv, 1.0), (q_at, dq, inv_root), (k_at, dk, inv_root)):
        d_pre = (acc[...] * scale * slope[:, base : base + width]).astype(BF16)
        d_normed = d_normed + dot_nt(d_pre, w_in[:, base : base + width])
    nr = normed[...]
    d_events = (
        grad[...].astype(F32)
        + (d_normed - row_mean(d_normed) - nr * row_mean(d_normed * nr)) * inv_in[:, 0:1]
    ).astype(BF16)

    zback[...] = dot_tn(
        look[...], jnp.concatenate([d_events[:, :half], d_events[:, half:]], axis=0)
    ).astype(BF16)
    second = exchange(zback, zret, a2_send, a2_recv)
    first.wait_send()
    ring_drain(nrm, x1_send, x1_recv)
    ring_drain(datt, x2_send, x2_recv)
    second.wait_recv()
    gsend[...] = dot(onehot[...], zret[...]).astype(BF16)

    @pl.loop(1, n_red)
    def _(k):
        c, where = red_peer(k)
        pltpu.make_async_remote_copy(
            src_ref=gsend.at[pl.ds(pl.multiple_of(c * part, part), part)],
            dst_ref=rsbuf.at[pl.ds(pl.multiple_of(mine * part, part), part)],
            send_sem=rs_send,
            recv_sem=rs_recv,
            device_id=where,
            device_id_type=MESH,
        ).start()

    mine_at = pl.ds(pl.multiple_of(mine * part, part), part)
    rsbuf[mine_at, :] = gsend[mine_at, :]
    others = pl.ds(0, (n_red - 1) * part)
    _, some = red_peer(1)
    reduced = pltpu.make_async_remote_copy(
        src_ref=gsend.at[others], dst_ref=rsbuf.at[others],
        send_sem=rs_send, recv_sem=rs_recv, device_id=some, device_id_type=MESH,
    )
    second.wait_send()
    reduced.wait_recv()
    total = rsbuf[0:part, :].astype(F32)
    for k in range(1, n_red):
        total = total + rsbuf[k * part : (k + 1) * part, :].astype(F32)
    agbuf[mine_at, :] = total.astype(BF16)

    @pl.loop(1, n_red)
    def _(k):
        _, where = red_peer(k)
        pltpu.make_async_remote_copy(
            src_ref=agbuf.at[mine_at],
            dst_ref=agbuf.at[mine_at],
            send_sem=ag_send,
            recv_sem=ag_recv,
            device_id=where,
            device_id_type=MESH,
        ).start()

    gathered = pltpu.make_async_remote_copy(
        src_ref=agbuf.at[others], dst_ref=agbuf.at[others],
        send_sem=ag_send, recv_sem=ag_recv, device_id=some, device_id_type=MESH,
    )
    reduced.wait_send()
    gathered.wait_recv()
    tgrad_ref[:, :half] = agbuf[:trows, :].astype(F32)
    tgrad_ref[:, half:] = agbuf[trows:, :].astype(F32)
    gathered.wait_send()


def per_device(table, served_rows, w_in, w_out, lookup_slots, block_users, out_grad):
    n_emb, n_bal, n_rep = (lax.axis_size(a) for a in ("emb", "bal", "rep"))
    trows, width = table.shape
    tok = lookup_slots.shape[1]
    half = width // 2
    steps = n_bal // 2
    slots = 2 * served_rows.shape[-1]
    served = served_rows.reshape(n_emb, 1, -1)
    idx = jnp.concatenate([served, served + trows], axis=1).reshape(1, slots)
    hd = width // HEADS
    vmem = pl.BlockSpec(memory_space=pltpu.VMEM)
    hbm = pl.BlockSpec(memory_space=pl.ANY)
    dma = pltpu.SemaphoreType.DMA
    n_red = n_bal * n_rep
    layer_out, table_grad = pl.pallas_call(
        functools.partial(layer_kernel, (n_emb, n_bal, n_rep)),
        out_shape=(
            jax.ShapeDtypeStruct((tok, width), BF16),
            jax.ShapeDtypeStruct((trows, width), F32),
        ),
        in_specs=[vmem, vmem, vmem, pl.BlockSpec(memory_space=pltpu.SMEM), hbm, hbm, hbm],
        out_specs=(vmem, vmem),
        scratch_shapes=[
            pltpu.VMEM((width, 4 * width), BF16),
            pltpu.VMEM((width, width), BF16),
            pltpu.VMEM((tok, width), BF16),
            pltpu.VMEM((slots, half), BF16),
            pltpu.VMEM((slots, half), BF16),
            pltpu.VMEM((slots, half), BF16),
            pltpu.VMEM((slots, half), BF16),
            pltpu.VMEM((2 * trows, slots), BF16),
            pltpu.VMEM((2 * tok, slots), BF16),
            pltpu.VMEM((tok, width), F32),
            pltpu.VMEM((tok, width), F32),
            pltpu.VMEM((tok, 128), F32),
            pltpu.VMEM((tok, 4 * width), BF16),
            pltpu.VMEM((tok, 4 * width), F32),
            pltpu.VMEM((n_bal, tok, width), BF16),
            pltpu.VMEM((n_bal, tok, width), BF16),
            pltpu.VMEM((n_bal, tok, 2 * width), BF16),
            pltpu.VMEM((n_bal, tok, width), BF16),
            pltpu.VMEM((n_bal, HEADS, tok, tok), BF16),
            pltpu.VMEM((n_bal, HEADS, tok, tok), F32),
            pltpu.VMEM((n_bal, HEADS, tok, tok), F32),
            pltpu.VMEM((tok, width), F32),
            pltpu.VMEM((tok, width), F32),
            pltpu.VMEM((tok, width), F32),
            pltpu.VMEM((tok, width), F32),
            pltpu.VMEM((2 * trows, half), BF16),
            pltpu.VMEM((2 * trows, half), BF16),
            pltpu.VMEM((2 * trows, half), BF16),
            dma((3,)),
            dma, dma,
            dma((2, steps, 2)), dma((2, steps, 2)),
            dma((2, steps, 2)), dma((2, steps, 2)),
            dma, dma, dma, dma, dma, dma,
        ],
        compiler_params=pltpu.CompilerParams(
            collective_id=0, has_side_effects=True, vmem_limit_bytes=48 * 1024 * 1024
        ),
    )(table, idx, lookup_slots[0], block_users, w_in, w_out, out_grad[0])
    return layer_out[None], table_grad


def solution(mesh):
    placed = (
        P("emb", None),
        P("emb", "bal", "rep", None),
        P(),
        P(),
        P(("emb", "rep"), "bal", None),
        P(("emb", "rep"), None),
        P(("emb", "rep"), "bal", None),
    )
    return jax.shard_map(
        per_device,
        mesh=mesh,
        in_specs=placed,
        out_specs=(P(("emb", "rep"), "bal", None), P("emb", None)),
        check_vma=False,
    )
```

```python
import functools
import math

import jax
import jax.numpy as jnp
from jax import lax
from jax.experimental import pallas as pl
from jax.experimental.pallas import tpu as pltpu
from jax.sharding import PartitionSpec as P

HEADS = 4
EPS = 1e-05
MESH = pl.DeviceIdType.MESH
F32 = jnp.float32
BF16 = jnp.bfloat16


def dot(a, b):
    return jnp.dot(a, b, preferred_element_type=F32)


def dot_nt(a, b):
    return lax.dot_general(a, b, (((1,), (1,)), ((), ())), preferred_element_type=F32)


def dot_tn(a, b):
    return lax.dot_general(a, b, (((0,), (0,)), ((), ())), preferred_element_type=F32)


def sigmoid(v):
    return 0.5 * jnp.tanh(0.5 * v) + 0.5


def silu(v):
    return v * sigmoid(v)


def silu_and_slope(v):
    s = sigmoid(v)
    y = v * s
    return y, s + y * (1.0 - s)


def row_mean(v):
    return jnp.mean(v, axis=-1, keepdims=True)


def layer_kernel(
    sizes,
    table_hbm, served_hbm, lookup_hbm, users_ref, w_in_hbm, w_out_hbm, grad_hbm,
    layer_ref, tgrad_ref,
    table, served, lookup, w_in, w_out, grad, zout, zin, zback, zret, onehot, look,
    events, normed, inv_in, act, slope, nrm, datt, kv, qall,
    wt, gt, gq, att, dq, dk, dv, d_mixed, normed_att, dn, gsend, cbuf, hsend, rsbuf, agbuf,
    load_sem, a1_send, a1_recv, x1_send, x1_recv, x2_send, x2_recv,
    a2_send, a2_recv, core_send, core_recv, rs_send, rs_recv, ag_send, ag_recv,
    fan_send, fan_recv,
):
    n_emb, n_bal, n_rep = sizes
    tok, width = grad.shape
    half = width // 2
    slab = zout.shape[0] // n_emb
    cap = slab // 2
    trows = table.shape[0]
    slots = n_emb * cap
    hd = width // HEADS
    inv_root = 1.0 / math.sqrt(hd)
    e = lax.axis_index("emb")
    b = lax.axis_index("bal")
    rep = lax.axis_index("rep")
    share = gsend.shape[0] // n_rep
    part = share // n_bal

    loads = [
        pltpu.make_async_copy(src, dst, load_sem.at[i])
        for i, (src, dst) in enumerate(
            (
                (served_hbm, served), (table_hbm, table), (lookup_hbm, lookup),
                (grad_hbm, grad), (w_out_hbm, w_out), (w_in_hbm, w_in),
            )
        )
    ]
    for load in loads:
        load.start()

    barrier = pltpu.get_barrier_semaphore()

    @pl.loop(1, n_emb)
    def _(k):
        pl.semaphore_signal(
            barrier, inc=1, device_id={"emb": lax.rem(e + k, n_emb)}, device_id_type=MESH
        )

    @pl.loop(1, n_bal)
    def _(k):
        pl.semaphore_signal(
            barrier, inc=1, device_id={"bal": lax.rem(b + k, n_bal)}, device_id_type=MESH
        )

    if n_rep == 2:
        pl.semaphore_signal(barrier, inc=1, device_id={"rep": 1 - rep}, device_id_type=MESH)

    def to_slabs(both):
        halves = [
            both[:, cols].reshape(n_emb, 1, cap, half)
            for cols in (slice(0, half), slice(half, width))
        ]
        return jnp.concatenate(halves, axis=1).reshape(2 * slots, half).astype(BF16)

    def from_slabs(slabs):
        apart = slabs.astype(F32).reshape(n_emb, 2, cap, half)
        return jnp.concatenate(
            [apart[:, h].reshape(slots, half) for h in range(2)], axis=1
        ).astype(BF16)

    loads[0].wait()
    rows_of = lax.broadcasted_iota(jnp.int32, onehot.shape, 0)
    onehot[...] = jnp.where(rows_of == served[...], 1.0, 0.0).astype(BF16)
    loads[1].wait()
    zout[...] = to_slabs(dot_tn(onehot[...], table[...]))

    pl.semaphore_wait(barrier, n_emb + n_bal + n_rep - 3)

    stride = 27 if n_emb % 3 else 1

    def exchange(src, dst, send, recv):
        own = pl.ds(pl.multiple_of(e * slab, slab), slab)

        @pl.loop(1, n_emb)
        def _(k):
            to = lax.rem(e + stride * k, n_emb)
            pltpu.make_async_remote_copy(
                src_ref=src.at[pl.ds(pl.multiple_of(to * slab, slab), slab)],
                dst_ref=dst.at[own],
                send_sem=send,
                recv_sem=recv,
                device_id={"emb": to},
                device_id_type=MESH,
            ).start()

        dst[own, :] = src[own, :]
        many = pl.ds(0, (n_emb - 1) * slab)
        return pltpu.make_async_remote_copy(
            src_ref=src.at[many],
            dst_ref=dst.at[many],
            send_sem=send,
            recv_sem=recv,
            device_id={"emb": lax.rem(e + 1, n_emb)},
            device_id_type=MESH,
        )

    first = exchange(zout, zin, a1_send, a1_recv)

    loads[2].wait()
    slot_of = lax.broadcasted_iota(jnp.int32, look.shape, 0)
    hit = (slot_of == lookup[0:1, :]) | (slot_of == lookup[1:2, :])
    look[...] = jnp.where(hit, 1.0, 0.0).astype(BF16)

    my_user = users_ref[0, b]
    count = jnp.int32(0)
    for k in range(n_bal):
        count = count + jnp.where(users_ref[0, k] == my_user, 1, 0)
    inv_len = jnp.float32(0.0)
    for k in range(1, n_bal + 1):
        inv_len = jnp.where(count == k, jnp.float32(1.0 / (k * tok)), inv_len)

    for load in loads[3:]:
        load.wait()
    d_mixed[...] = dot_nt(grad[...], w_out[...])

    first.wait_recv()
    ev = dot_tn(look[...], from_slabs(zin[...]))
    events[...] = ev
    centered = ev - row_mean(ev)
    inv = lax.rsqrt(row_mean(centered * centered) + EPS)
    inv_in[...] = jnp.broadcast_to(inv, inv_in.shape)
    normed[...] = centered * inv
    nrm[0] = normed[...].astype(BF16)

    rows = tok // 2
    steps = n_bal // 2
    right = lax.rem(b + 1, n_bal)
    left = lax.rem(b + n_bal - 1, n_bal)

    def hop(buf, send, recv, way, step, c):
        if way == 0:
            src, dst, to = lax.rem(n_bal - step, n_bal), n_bal - 1 - step, right
        else:
            src, dst, to = step, step + 1, left
        piece = pl.ds(c * rows, rows)
        return pltpu.make_async_remote_copy(
            src_ref=buf.at[src, piece],
            dst_ref=buf.at[dst, piece],
            send_sem=send.at[way, step, c],
            recv_sem=recv.at[way, step, c],
            device_id={"bal": to},
            device_id_type=MESH,
        )

    lanes = [(way, c) for c in range(2) for way in range(2)]

    def ring_start(buf, send, recv):
        for way, c in lanes:
            if steps > 1 or way == c:
                hop(buf, send, recv, way, 0, c).start()

    def ring_rest(buf, send, recv, own_work, on_block):
        @pl.loop(0, steps + 1)
        def _(step):
            for c in range(2):
                for way in range(2):
                    last = steps - 1 if way == c else steps - 2

                    @pl.when(step <= last)
                    def _():
                        hop(buf, send, recv, way, step, c).wait_recv()

                    @pl.when(step + 1 <= last)
                    def _():
                        hop(buf, send, recv, way, step + 1, c).start()

                @pl.when(step == 0)
                def _():
                    own_work[c]()

            @pl.when(step > 0)
            def _():
                @pl.loop(0, 2)
                def _(k):
                    @pl.when((k == 0) | (step < steps))
                    def _():
                        on_block(jnp.where(k == 0, n_bal - step, step))

    def ring_drain(buf, send, recv):
        @pl.loop(0, steps)
        def _(step):
            for way, c in lanes:
                last = steps - 1 if way == c else steps - 2

                @pl.when(step <= last)
                def _():
                    hop(buf, send, recv, way, step, c).wait_send()

    ring_start(nrm, x1_send, x1_recv)
    v_at, q_at, k_at = width, 2 * width, 3 * width

    def head(h, base=0):
        return slice(base + h * hd, base + (h + 1) * hd)

    def project(*columns):
        for base in columns:
            cols = slice(base, base + width)
            a, s = silu_and_slope(dot(nrm[0], w_in[:, cols]))
            act[:, cols] = a.astype(BF16)
            slope[:, cols] = s

    def own_pair():
        project(0)
        tri_row = lax.broadcasted_iota(jnp.int32, (tok, tok), 0)
        tri_col = lax.broadcasted_iota(jnp.int32, (tok, tok), 1)
        for h in range(HEADS):
            q, k, v = act[:, head(h, q_at)], act[:, head(h, k_at)], act[:, head(h, v_at)]
            y, g = silu_and_slope(dot_nt(q, k) * inv_root)
            keep = tri_row >= tri_col
            att[:, head(h)] = dot(jnp.where(keep, y * inv_len, 0.0).astype(BF16), v)
            gq[0, h] = jnp.where(keep, g * inv_len, 0.0)
            y, g = silu_and_slope(dot_nt(k, q) * inv_root)
            keep = tri_row <= tri_col
            wt[0, h] = jnp.where(keep, y * inv_len, 0.0).astype(BF16)
            gt[0, h] = jnp.where(keep, g * inv_len, 0.0)

    def seen(j):
        return jnp.where(users_ref[0, j] == my_user, inv_len, jnp.float32(0.0))

    def forward_block(r):
        j = lax.rem(b + r, n_bal)
        f = seen(j)

        @pl.when(j < b)
        def _():
            x = nrm[r]
            kv[r, :, :width] = silu(dot(x, w_in[:, v_at : v_at + width])).astype(BF16)
            kv[r, :, width:] = silu(dot(x, w_in[:, k_at : k_at + width])).astype(BF16)
            for h in range(HEADS):
                k = kv[r, :, head(h, width)]
                y, g = silu_and_slope(dot_nt(act[:, head(h, q_at)], k) * inv_root)
                gq[r, h] = g * f
                att[:, head(h)] += dot((y * f).astype(BF16), kv[r, :, head(h)])

        @pl.when(j > b)
        def _():
            qall[r] = silu(dot(nrm[r], w_in[:, q_at : q_at + width])).astype(BF16)
            for h in range(HEADS):
                y, g = silu_and_slope(
                    dot_nt(act[:, head(h, k_at)], qall[r, :, head(h)]) * inv_root
                )
                gt[r, h] = g * f
                wt[r, h] = (y * f).astype(BF16)

    ring_rest(
        nrm, x1_send, x1_recv, (lambda: project(q_at, k_at, v_at), own_pair), forward_block
    )

    at = att[...]
    centered = at - row_mean(at)
    inv_att = lax.rsqrt(row_mean(centered * centered) + EPS)
    na = centered * inv_att
    normed_att[...] = na
    d_gated = d_mixed[...] * act[:, :width].astype(F32)
    d_att = (
        (d_gated - row_mean(d_gated) - na * row_mean(d_gated * na)) * inv_att
    ).astype(BF16)
    datt[0] = d_att
    ring_start(datt, x2_send, x2_recv)

    def own_pair_back():
        for h in range(HEADS):
            q, k, v = act[:, head(h, q_at)], act[:, head(h, k_at)], act[:, head(h, v_at)]
            d = datt[0, :, head(h)]
            ds = (dot_nt(d, v) * gq[0, h]).astype(BF16)
            dq[:, head(h)] = dot(ds, k)
            dv[:, head(h)] = dot(wt[0, h], d)
            dst = (dot_nt(v, d) * gt[0, h]).astype(BF16)
            dk[:, head(h)] = dot(dst, q)

    def layer_and_gate():
        mixed = (normed_att[...] * act[:, :width].astype(F32)).astype(BF16)
        layer_ref[...] = (events[...] + dot(mixed, w_out[...])).astype(BF16)
        d_pre = (d_mixed[...] * normed_att[...] * slope[:, :width]).astype(BF16)
        dn[...] = dot_nt(d_pre, w_in[:, :width])

    def backward_block(r):
        j = lax.rem(b + r, n_bal)

        @pl.when(j < b)
        def _():
            for h in range(HEADS):
                ds = (dot_nt(datt[0, :, head(h)], kv[r, :, head(h)]) * gq[r, h]).astype(BF16)
                dq[:, head(h)] += dot(ds, kv[r, :, head(h, width)])

        @pl.when(j > b)
        def _():
            for h in range(HEADS):
                d = datt[r, :, head(h)]
                dv[:, head(h)] += dot(wt[r, h], d)
                dst = (dot_nt(act[:, head(h, v_at)], d) * gt[r, h]).astype(BF16)
                dk[:, head(h)] += dot(dst, qall[r, :, head(h)])

    ring_rest(datt, x2_send, x2_recv, (own_pair_back, layer_and_gate), backward_block)

    d_normed = dn[...]
    for base, acc, scale in ((v_at, dv, 1.0), (q_at, dq, inv_root), (k_at, dk, inv_root)):
        d_pre = (acc[...] * scale * slope[:, base : base + width]).astype(BF16)
        d_normed = d_normed + dot_nt(d_pre, w_in[:, base : base + width])
    nr = normed[...]
    d_events = (
        grad[...].astype(F32)
        + (d_normed - row_mean(d_normed) - nr * row_mean(d_normed * nr)) * inv_in[:, 0:1]
    ).astype(BF16)

    zback[...] = to_slabs(dot(look[...], d_events))
    second = exchange(zback, zret, a2_send, a2_recv)
    first.wait_send()
    ring_drain(nrm, x1_send, x1_recv)
    ring_drain(datt, x2_send, x2_recv)
    second.wait_recv()
    grads = dot(onehot[...], from_slabs(zret[...])).astype(BF16)
    gsend[:trows, :] = grads[:, :half]
    gsend[trows:, :] = grads[:, half:]

    ours = pl.ds(pl.multiple_of(rep * share, share), share)
    own_part = pl.ds(pl.multiple_of(b * part, part), part)
    if n_rep == 2:
        theirs = pl.ds(pl.multiple_of((1 - rep) * share, share), share)
        swap = pltpu.make_async_remote_copy(
            src_ref=gsend.at[theirs], dst_ref=cbuf, send_sem=core_send, recv_sem=core_recv,
            device_id={"rep": 1 - rep}, device_id_type=MESH,
        )
        swap.start()
        swap.wait_recv()
        hsend[...] = (gsend[ours, :].astype(F32) + cbuf[...].astype(F32)).astype(BF16)
    else:
        hsend[...] = gsend[...]

    @pl.loop(1, n_bal)
    def _(k):
        c = lax.rem(b + k, n_bal)
        pltpu.make_async_remote_copy(
            src_ref=hsend.at[pl.ds(pl.multiple_of(c * part, part), part)],
            dst_ref=rsbuf.at[own_part],
            send_sem=rs_send,
            recv_sem=rs_recv,
            device_id={"bal": c},
            device_id_type=MESH,
        ).start()

    rsbuf[own_part, :] = hsend[own_part, :]
    others = pl.ds(0, (n_bal - 1) * part)
    reduced = pltpu.make_async_remote_copy(
        src_ref=hsend.at[others], dst_ref=rsbuf.at[others],
        send_sem=rs_send, recv_sem=rs_recv, device_id={"bal": right}, device_id_type=MESH,
    )
    second.wait_send()
    reduced.wait_recv()
    total = rsbuf[0:part, :].astype(F32)
    for k in range(1, n_bal):
        total = total + rsbuf[k * part : (k + 1) * part, :].astype(F32)
    mine_at = pl.ds(pl.multiple_of(rep * share + b * part, part), part)
    agbuf[mine_at, :] = total.astype(BF16)

    @pl.loop(1, n_bal)
    def _(k):
        pltpu.make_async_remote_copy(
            src_ref=agbuf.at[mine_at],
            dst_ref=agbuf.at[mine_at],
            send_sem=ag_send,
            recv_sem=ag_recv,
            device_id={"bal": lax.rem(b + k, n_bal)},
            device_id_type=MESH,
        ).start()

    gathered = pltpu.make_async_remote_copy(
        src_ref=agbuf.at[others], dst_ref=agbuf.at[others],
        send_sem=ag_send, recv_sem=ag_recv, device_id={"bal": right}, device_id_type=MESH,
    )
    reduced.wait_send()
    gathered.wait_recv()
    if n_rep == 2:
        fan = pltpu.make_async_remote_copy(
            src_ref=agbuf.at[ours], dst_ref=agbuf.at[ours], send_sem=fan_send,
            recv_sem=fan_recv, device_id={"rep": 1 - rep}, device_id_type=MESH,
        )
        fan.start()
        swap.wait_send()
        fan.wait_recv()
    tgrad_ref[:, :half] = agbuf[:trows, :]
    tgrad_ref[:, half:] = agbuf[trows:, :]
    gathered.wait_send()
    if n_rep == 2:
        fan.wait_send()


def per_device(table, served_rows, w_in, w_out, lookup_slots, block_users, out_grad):
    n_emb, n_bal, n_rep = (lax.axis_size(a) for a in ("emb", "bal", "rep"))
    trows, width = table.shape
    tok = lookup_slots.shape[1]
    half = width // 2
    steps = n_bal // 2
    slots = 2 * served_rows.shape[-1]
    hd = width // HEADS
    vmem = pl.BlockSpec(memory_space=pltpu.VMEM)
    hbm = pl.BlockSpec(memory_space=pltpu.HBM)
    dma = pltpu.SemaphoreType.DMA
    share = 2 * trows // n_rep
    layer_out, table_grad = pl.pallas_call(
        functools.partial(layer_kernel, (n_emb, n_bal, n_rep)),
        out_shape=(
            jax.ShapeDtypeStruct((tok, width), BF16),
            jax.ShapeDtypeStruct((trows, width), BF16),
        ),
        in_specs=[hbm, hbm, hbm, pl.BlockSpec(memory_space=pltpu.SMEM), hbm, hbm, hbm],
        out_specs=(vmem, vmem),
        scratch_shapes=[
            pltpu.VMEM((trows, width), BF16),
            pltpu.VMEM((1, slots // 2), jnp.int32),
            pltpu.VMEM((2, tok), jnp.int32),
            pltpu.VMEM((width, 4 * width), BF16),
            pltpu.VMEM((width, width), BF16),
            pltpu.VMEM((tok, width), BF16),
            pltpu.VMEM((slots, half), BF16),
            pltpu.VMEM((slots, half), BF16),
            pltpu.VMEM((slots, half), BF16),
            pltpu.VMEM((slots, half), BF16),
            pltpu.VMEM((trows, slots // 2), BF16),
            pltpu.VMEM((slots // 2, tok), BF16),
            pltpu.VMEM((tok, width), F32),
            pltpu.VMEM((tok, width), F32),
            pltpu.VMEM((tok, 128), F32),
            pltpu.VMEM((tok, 4 * width), BF16),
            pltpu.VMEM((tok, 4 * width), F32),
            pltpu.VMEM((n_bal, tok, width), BF16),
            pltpu.VMEM((n_bal, tok, width), BF16),
            pltpu.VMEM((n_bal, tok, 2 * width), BF16),
            pltpu.VMEM((n_bal, tok, width), BF16),
            pltpu.VMEM((n_bal, HEADS, tok, tok), BF16),
            pltpu.VMEM((n_bal, HEADS, tok, tok), F32),
            pltpu.VMEM((n_bal, HEADS, tok, tok), F32),
            pltpu.VMEM((tok, width), F32),
            pltpu.VMEM((tok, width), F32),
            pltpu.VMEM((tok, width), F32),
            pltpu.VMEM((tok, width), F32),
            pltpu.VMEM((tok, width), F32),
            pltpu.VMEM((tok, width), F32),
            pltpu.VMEM((tok, width), F32),
            pltpu.VMEM((2 * trows, half), BF16),
            pltpu.VMEM((share, half), BF16),
            pltpu.VMEM((share, half), BF16),
            pltpu.VMEM((share, half), BF16),
            pltpu.VMEM((2 * trows, half), BF16),
            dma((6,)),
            dma, dma,
            dma((2, steps, 2)), dma((2, steps, 2)),
            dma((2, steps, 2)), dma((2, steps, 2)),
            dma, dma, dma, dma, dma, dma, dma, dma, dma, dma,
        ],
        compiler_params=pltpu.CompilerParams(
            collective_id=0, has_side_effects=True, vmem_limit_bytes=56 * 1024 * 1024
        ),
    )(
        table, served_rows.reshape(1, -1), lookup_slots[0].T, block_users, w_in, w_out, out_grad[0],
    )
    return layer_out[None], table_grad.astype(F32)


def solution(mesh):
    placed = (
        P("emb", None),
        P("emb", "bal", "rep", None),
        P(),
        P(),
        P(("emb", "rep"), "bal", None),
        P(("emb", "rep"), None),
        P(("emb", "rep"), "bal", None),
    )
    return jax.shard_map(
        per_device,
        mesh=mesh,
        in_specs=placed,
        out_specs=(P(("emb", "rep"), "bal", None), P("emb", None)),
        check_vma=False,
    )
```

```python
import functools
import math

import jax
import jax.numpy as jnp
from jax import lax
from jax.experimental import pallas as pl
from jax.experimental.pallas import tpu as pltpu
from jax.sharding import PartitionSpec as P

HEADS = 4
EPS = 1e-05
MESH = pl.DeviceIdType.MESH
F32 = jnp.float32
BF16 = jnp.bfloat16


def dot(a, b):
    return jnp.dot(a, b, preferred_element_type=F32)


def dot_nt(a, b):
    return lax.dot_general(a, b, (((1,), (1,)), ((), ())), preferred_element_type=F32)


def dot_tn(a, b):
    return lax.dot_general(a, b, (((0,), (0,)), ((), ())), preferred_element_type=F32)


def sigmoid(v):
    return 0.5 * jnp.tanh(0.5 * v) + 0.5


def silu(v):
    return v * sigmoid(v)


def silu_and_slope(v):
    s = sigmoid(v)
    y = v * s
    return y, s + y * (1.0 - s)


def row_mean(v):
    return jnp.mean(v, axis=-1, keepdims=True)


def layer_kernel(
    sizes,
    table_hbm, served_hbm, lookup_hbm, users_ref, w_in_hbm, w_out_hbm, grad_hbm,
    layer_ref, tgrad_ref,
    table, served, lookup, w_in, w_out, grad, zout, zin, zback, zret, onehot, look,
    events, normed, inv_in, act, slope, evs, nrm, datt, kv, qall,
    wt, gt, gq, att, dq, dk, dv, d_mixed, normed_att, dn, gsend, cbuf, hsend, rsbuf, agbuf,
    load_sem, a1_send, a1_recv, x1_send, x1_recv, x2_send, x2_recv,
    a2_send, a2_recv, core_send, core_recv, rs_send, rs_recv, ag_send, ag_recv,
    fan_send, fan_recv,
):
    n_emb, n_bal, n_rep = sizes
    tok, width = grad.shape
    half = width // 2
    slab = zout.shape[0] // n_emb
    cap = slab // 2
    trows = table.shape[0]
    slots = n_emb * cap
    hd = width // HEADS
    inv_root = 1.0 / math.sqrt(hd)
    e = lax.axis_index("emb")
    b = lax.axis_index("bal")
    rep = lax.axis_index("rep")
    share = trows // n_rep
    part = share // n_bal
    quarter = half // 2

    loads = [
        pltpu.make_async_copy(src, dst, load_sem.at[i])
        for i, (src, dst) in enumerate(
            (
                (served_hbm, served), (table_hbm, table), (lookup_hbm, lookup),
                (grad_hbm, grad), (w_out_hbm, w_out), (w_in_hbm, w_in),
            )
        )
    ]
    for load in loads:
        load.start()

    barrier = pltpu.get_barrier_semaphore()

    @pl.loop(1, n_emb)
    def _(k):
        pl.semaphore_signal(
            barrier, inc=1, device_id={"emb": lax.rem(e + k, n_emb)}, device_id_type=MESH
        )

    @pl.loop(1, n_bal)
    def _(k):
        pl.semaphore_signal(
            barrier, inc=1, device_id={"bal": lax.rem(b + k, n_bal)}, device_id_type=MESH
        )

    if n_rep == 2:
        pl.semaphore_signal(barrier, inc=1, device_id={"rep": 1 - rep}, device_id_type=MESH)

    chunks = [pl.ds(c * quarter, quarter) for c in range(2)]
    wide = [pl.ds(c * half, half) for c in range(2)]

    def to_slabs(rows_f32):
        copies = [
            jnp.concatenate(
                [
                    rows_f32[:, c * half + h * quarter : c * half + (h + 1) * quarter]
                    for c in range(2)
                ],
                axis=1,
            ).reshape(n_emb, 1, cap, half)
            for h in range(2)
        ]
        return jnp.concatenate(copies, axis=1).reshape(2 * slots, half).astype(BF16)

    def from_slabs(chunk):
        apart = chunk.astype(F32).reshape(n_emb, 2, cap, quarter)
        return jnp.concatenate(
            [apart[:, h].reshape(slots, quarter) for h in range(2)], axis=1
        ).astype(BF16)

    loads[0].wait()
    rows_of = lax.broadcasted_iota(jnp.int32, onehot.shape, 0)
    onehot[...] = jnp.where(rows_of == served[...], 1.0, 0.0).astype(BF16)
    loads[1].wait()
    zout[...] = to_slabs(dot_tn(onehot[...], table[...]))

    pl.semaphore_wait(barrier, n_emb + n_bal + n_rep - 3)

    stride = 27 if n_emb % 3 else 1

    def exchange(src, dst, send, recv):
        own = pl.ds(pl.multiple_of(e * slab, slab), slab)
        many = pl.ds(0, (n_emb - 1) * slab)
        waits = []
        for c in range(2):
            @pl.loop(1, n_emb)
            def _(k):
                to = lax.rem(e + stride * k, n_emb)
                pltpu.make_async_remote_copy(
                    src_ref=src.at[pl.ds(pl.multiple_of(to * slab, slab), slab), chunks[c]],
                    dst_ref=dst.at[own, chunks[c]],
                    send_sem=send.at[c],
                    recv_sem=recv.at[c],
                    device_id={"emb": to},
                    device_id_type=MESH,
                ).start()

            waits.append(
                pltpu.make_async_remote_copy(
                    src_ref=src.at[many, chunks[c]],
                    dst_ref=dst.at[many, chunks[c]],
                    send_sem=send.at[c],
                    recv_sem=recv.at[c],
                    device_id={"emb": lax.rem(e + 1, n_emb)},
                    device_id_type=MESH,
                )
            )
        dst[own, :] = src[own, :]
        return waits

    first = exchange(zout, zin, a1_send, a1_recv)

    loads[2].wait()
    slot_of = lax.broadcasted_iota(jnp.int32, look.shape, 0)
    hit = (slot_of == lookup[0:1, :]) | (slot_of == lookup[1:2, :])
    look[...] = jnp.where(hit, 1.0, 0.0).astype(BF16)

    my_user = users_ref[0, b]
    count = jnp.int32(0)
    for k in range(n_bal):
        count = count + jnp.where(users_ref[0, k] == my_user, 1, 0)
    inv_len = jnp.float32(0.0)
    for k in range(1, n_bal + 1):
        inv_len = jnp.where(count == k, jnp.float32(1.0 / (k * tok)), inv_len)

    for load in loads[3:]:
        load.wait()
    d_mixed[...] = dot_nt(grad[...], w_out[...])

    rows = tok // 2
    steps = n_bal // 2
    right = lax.rem(b + 1, n_bal)
    left = lax.rem(b + n_bal - 1, n_bal)

    def hop(ring, way, step, c):
        buf, lanes_of, send, recv = ring
        if way == 0:
            src, dst, to = lax.rem(n_bal - step, n_bal), n_bal - 1 - step, right
        else:
            src, dst, to = step, step + 1, left
        piece = pl.ds(c * rows, rows)
        return pltpu.make_async_remote_copy(
            src_ref=buf.at[src, piece, lanes_of],
            dst_ref=buf.at[dst, piece, lanes_of],
            send_sem=send.at[way, step, c],
            recv_sem=recv.at[way, step, c],
            device_id={"bal": to},
            device_id_type=MESH,
        )

    lanes = [(way, c) for c in range(2) for way in range(2)]

    def ring_start(ring):
        for way, c in lanes:
            if steps > 1 or way == c:
                hop(ring, way, 0, c).start()

    def ring_rest(ring, own_work, on_block):
        @pl.loop(0, steps + 1 if on_block else steps)
        def _(step):
            for c in range(2):
                for way in range(2):
                    last = steps - 1 if way == c else steps - 2

                    @pl.when(step <= last)
                    def _():
                        hop(ring, way, step, c).wait_recv()

                    @pl.when(step + 1 <= last)
                    def _():
                        hop(ring, way, step + 1, c).start()

                if own_work:
                    @pl.when(step == 0)
                    def _():
                        own_work[c]()

            if on_block is None:
                return

            @pl.when(step > 0)
            def _():
                @pl.loop(0, 2)
                def _(k):
                    @pl.when((k == 0) | (step < steps))
                    def _():
                        on_block(jnp.where(k == 0, n_bal - step, step))

    def ring_drain(ring):
        @pl.loop(0, steps)
        def _(step):
            for way, c in lanes:
                last = steps - 1 if way == c else steps - 2

                @pl.when(step <= last)
                def _():
                    hop(ring, way, step, c).wait_send()

    rings = [(evs, wide[c], x1_send.at[c], x1_recv.at[c]) for c in range(2)]
    whole = (datt, slice(None), x2_send, x2_recv)

    def take_events(c):
        first[c].wait_recv()
        ev = dot_tn(look[...], from_slabs(zin[:, chunks[c]]))
        events[:, wide[c]] = ev
        evs[0, :, wide[c]] = ev.astype(BF16)
        ring_start(rings[c])

    take_events(0)
    ring_rest(rings[0], None, None)
    take_events(1)

    def normalized(ev):
        centered = ev - row_mean(ev)
        inv = lax.rsqrt(row_mean(centered * centered) + EPS)
        return centered * inv, inv

    v_at, q_at, k_at = width, 2 * width, 3 * width

    def head(h, base=0):
        return slice(base + h * hd, base + (h + 1) * hd)

    def own_rows():
        n, inv = normalized(events[...])
        inv_in[...] = jnp.broadcast_to(inv, inv_in.shape)
        normed[...] = n
        nrm[...] = n.astype(BF16)
        project(q_at, k_at, v_at)

    def project(*columns):
        for base in columns:
            cols = slice(base, base + width)
            a, s = silu_and_slope(dot(nrm[...], w_in[:, cols]))
            act[:, cols] = a.astype(BF16)
            slope[:, cols] = s

    def own_pair():
        project(0)
        tri_row = lax.broadcasted_iota(jnp.int32, (tok, tok), 0)
        tri_col = lax.broadcasted_iota(jnp.int32, (tok, tok), 1)
        for h in range(HEADS):
            q, k, v = act[:, head(h, q_at)], act[:, head(h, k_at)], act[:, head(h, v_at)]
            y, g = silu_and_slope(dot_nt(q, k) * inv_root)
            keep = tri_row >= tri_col
            att[:, head(h)] = dot(jnp.where(keep, y * inv_len, 0.0).astype(BF16), v)
            gq[0, h] = jnp.where(keep, g * inv_len, 0.0)
            y, g = silu_and_slope(dot_nt(k, q) * inv_root)
            keep = tri_row <= tri_col
            wt[0, h] = jnp.where(keep, y * inv_len, 0.0).astype(BF16)
            gt[0, h] = jnp.where(keep, g * inv_len, 0.0)

    def seen(j):
        return jnp.where(users_ref[0, j] == my_user, inv_len, jnp.float32(0.0))

    def forward_block(r):
        j = lax.rem(b + r, n_bal)
        f = seen(j)

        @pl.when(j < b)
        def _():
            x = normalized(evs[r].astype(F32))[0].astype(BF16)
            kv[r, :, :width] = silu(dot(x, w_in[:, v_at : v_at + width])).astype(BF16)
            kv[r, :, width:] = silu(dot(x, w_in[:, k_at : k_at + width])).astype(BF16)
            for h in range(HEADS):
                k = kv[r, :, head(h, width)]
                y, g = silu_and_slope(dot_nt(act[:, head(h, q_at)], k) * inv_root)
                gq[r, h] = g * f
                att[:, head(h)] += dot((y * f).astype(BF16), kv[r, :, head(h)])

        @pl.when(j > b)
        def _():
            x = normalized(evs[r].astype(F32))[0].astype(BF16)
            qall[r] = silu(dot(x, w_in[:, q_at : q_at + width])).astype(BF16)
            for h in range(HEADS):
                y, g = silu_and_slope(
                    dot_nt(act[:, head(h, k_at)], qall[r, :, head(h)]) * inv_root
                )
                gt[r, h] = g * f
                wt[r, h] = (y * f).astype(BF16)

    ring_rest(rings[1], (own_rows, own_pair), forward_block)

    na, inv_att = normalized(att[...])
    normed_att[...] = na
    d_gated = d_mixed[...] * act[:, :width].astype(F32)
    d_att = (
        (d_gated - row_mean(d_gated) - na * row_mean(d_gated * na)) * inv_att
    ).astype(BF16)
    datt[0] = d_att
    ring_start(whole)

    def own_pair_back():
        for h in range(HEADS):
            q, k, v = act[:, head(h, q_at)], act[:, head(h, k_at)], act[:, head(h, v_at)]
            d = datt[0, :, head(h)]
            ds = (dot_nt(d, v) * gq[0, h]).astype(BF16)
            dq[:, head(h)] = dot(ds, k)
            dv[:, head(h)] = dot(wt[0, h], d)
            dst = (dot_nt(v, d) * gt[0, h]).astype(BF16)
            dk[:, head(h)] = dot(dst, q)

    def layer_and_gate():
        mixed = (normed_att[...] * act[:, :width].astype(F32)).astype(BF16)
        layer_ref[...] = (events[...] + dot(mixed, w_out[...])).astype(BF16)
        d_pre = (d_mixed[...] * normed_att[...] * slope[:, :width]).astype(BF16)
        dn[...] = dot_nt(d_pre, w_in[:, :width])

    def backward_block(r):
        j = lax.rem(b + r, n_bal)

        @pl.when(j < b)
        def _():
            for h in range(HEADS):
                ds = (dot_nt(datt[0, :, head(h)], kv[r, :, head(h)]) * gq[r, h]).astype(BF16)
                dq[:, head(h)] += dot(ds, kv[r, :, head(h, width)])

        @pl.when(j > b)
        def _():
            for h in range(HEADS):
                d = datt[r, :, head(h)]
                dv[:, head(h)] += dot(wt[r, h], d)
                dst = (dot_nt(act[:, head(h, v_at)], d) * gt[r, h]).astype(BF16)
                dk[:, head(h)] += dot(dst, qall[r, :, head(h)])

    ring_rest(whole, (own_pair_back, layer_and_gate), backward_block)

    d_normed = dn[...]
    for base, acc, scale in ((v_at, dv, 1.0), (q_at, dq, inv_root), (k_at, dk, inv_root)):
        d_pre = (acc[...] * scale * slope[:, base : base + width]).astype(BF16)
        d_normed = d_normed + dot_nt(d_pre, w_in[:, base : base + width])
    nr = normed[...]
    d_events = (
        grad[...].astype(F32)
        + (d_normed - row_mean(d_normed) - nr * row_mean(d_normed * nr)) * inv_in[:, 0:1]
    ).astype(BF16)

    zback[...] = to_slabs(dot(look[...], d_events))
    second = exchange(zback, zret, a2_send, a2_recv)
    for c in range(2):
        first[c].wait_send()
        ring_drain(rings[c])
    ring_drain(whole)

    ours = pl.ds(pl.multiple_of(rep * share, share), share)
    theirs = pl.ds(pl.multiple_of((n_rep - 1 - rep) * share, share), share)
    own_part = pl.ds(pl.multiple_of(b * part, part), part)
    mine_at = pl.ds(pl.multiple_of(rep * share + b * part, part), part)
    others = pl.ds(0, (n_bal - 1) * part)
    other_core = {"rep": n_rep - 1 - rep}
    pending = []

    def remote(src, dst, send, recv, where):
        return pltpu.make_async_remote_copy(
            src_ref=src, dst_ref=dst, send_sem=send, recv_sem=recv,
            device_id=where, device_id_type=MESH,
        )

    def reduce_chunk(c):
        second[c].wait_recv()
        gsend[c] = dot(onehot[...], from_slabs(zret[:, chunks[c]])).astype(BF16)
        if n_rep == 2:
            swap = remote(
                gsend.at[c, theirs], cbuf.at[c], core_send.at[c], core_recv.at[c], other_core
            )
            swap.start()
            pending.append(swap)
            swap.wait_recv()
            hsend[c] = (gsend[c, ours, :].astype(F32) + cbuf[c].astype(F32)).astype(BF16)
        else:
            hsend[c] = gsend[c]

        @pl.loop(1, n_bal)
        def _(k):
            to = lax.rem(b + k, n_bal)
            remote(
                hsend.at[c, pl.ds(pl.multiple_of(to * part, part), part)],
                rsbuf.at[c, own_part], rs_send.at[c], rs_recv.at[c], {"bal": to},
            ).start()

        rsbuf[c, own_part, :] = hsend[c, own_part, :]
        reduced = remote(
            hsend.at[c, others], rsbuf.at[c, others], rs_send.at[c], rs_recv.at[c],
            {"bal": right},
        )
        pending.append(reduced)
        reduced.wait_recv()
        total = rsbuf[c, 0:part, :].astype(F32)
        for k in range(1, n_bal):
            total = total + rsbuf[c, k * part : (k + 1) * part, :].astype(F32)
        agbuf[c, mine_at, :] = total.astype(BF16)

        @pl.loop(1, n_bal)
        def _(k):
            remote(
                agbuf.at[c, mine_at], agbuf.at[c, mine_at], ag_send.at[c], ag_recv.at[c],
                {"bal": lax.rem(b + k, n_bal)},
            ).start()

    def finish_chunk(c):
        gathered = remote(
            agbuf.at[c, others], agbuf.at[c, others], ag_send.at[c], ag_recv.at[c],
            {"bal": right},
        )
        gathered.wait_recv()
        pending.append(gathered)
        if n_rep == 2:
            fan = remote(
                agbuf.at[c, ours], agbuf.at[c, ours], fan_send.at[c], fan_recv.at[c], other_core
            )
            fan.start()
            pending.append(fan)
            return fan

    reduce_chunk(0)
    fan0 = finish_chunk(0)
    reduce_chunk(1)
    fan1 = finish_chunk(1)
    for c, fan in enumerate((fan0, fan1)):
        if fan is not None:
            fan.wait_recv()
        tgrad_ref[:, wide[c]] = agbuf[c]
    for copy in second + pending:
        copy.wait_send()


def per_device(table, served_rows, w_in, w_out, lookup_slots, block_users, out_grad):
    n_emb, n_bal, n_rep = (lax.axis_size(a) for a in ("emb", "bal", "rep"))
    trows, width = table.shape
    tok = lookup_slots.shape[1]
    half = width // 2
    steps = n_bal // 2
    slots = 2 * served_rows.shape[-1]
    hd = width // HEADS
    vmem = pl.BlockSpec(memory_space=pltpu.VMEM)
    hbm = pl.BlockSpec(memory_space=pltpu.HBM)
    dma = pltpu.SemaphoreType.DMA
    share = trows // n_rep
    layer_out, table_grad = pl.pallas_call(
        functools.partial(layer_kernel, (n_emb, n_bal, n_rep)),
        out_shape=(
            jax.ShapeDtypeStruct((tok, width), BF16),
            jax.ShapeDtypeStruct((trows, width), BF16),
        ),
        in_specs=[hbm, hbm, hbm, pl.BlockSpec(memory_space=pltpu.SMEM), hbm, hbm, hbm],
        out_specs=(vmem, vmem),
        scratch_shapes=[
            pltpu.VMEM((trows, width), BF16),
            pltpu.VMEM((1, slots // 2), jnp.int32),
            pltpu.VMEM((2, tok), jnp.int32),
            pltpu.VMEM((width, 4 * width), BF16),
            pltpu.VMEM((width, width), BF16),
            pltpu.VMEM((tok, width), BF16),
            pltpu.VMEM((slots, half), BF16),
            pltpu.VMEM((slots, half), BF16),
            pltpu.VMEM((slots, half), BF16),
            pltpu.VMEM((slots, half), BF16),
            pltpu.VMEM((trows, slots // 2), BF16),
            pltpu.VMEM((slots // 2, tok), BF16),
            pltpu.VMEM((tok, width), F32),
            pltpu.VMEM((tok, width), F32),
            pltpu.VMEM((tok, 128), F32),
            pltpu.VMEM((tok, 4 * width), BF16),
            pltpu.VMEM((tok, 4 * width), F32),
            pltpu.VMEM((n_bal, tok, width), BF16),
            pltpu.VMEM((tok, width), BF16),
            pltpu.VMEM((n_bal, tok, width), BF16),
            pltpu.VMEM((n_bal, tok, 2 * width), BF16),
            pltpu.VMEM((n_bal, tok, width), BF16),
            pltpu.VMEM((n_bal, HEADS, tok, tok), BF16),
            pltpu.VMEM((n_bal, HEADS, tok, tok), F32),
            pltpu.VMEM((n_bal, HEADS, tok, tok), F32),
            pltpu.VMEM((tok, width), F32),
            pltpu.VMEM((tok, width), F32),
            pltpu.VMEM((tok, width), F32),
            pltpu.VMEM((tok, width), F32),
            pltpu.VMEM((tok, width), F32),
            pltpu.VMEM((tok, width), F32),
            pltpu.VMEM((tok, width), F32),
            pltpu.VMEM((2, trows, half), BF16),
            pltpu.VMEM((2, share, half), BF16),
            pltpu.VMEM((2, share, half), BF16),
            pltpu.VMEM((2, share, half), BF16),
            pltpu.VMEM((2, trows, half), BF16),
            dma((6,)),
            dma((2,)), dma((2,)),
            dma((2, 2, steps, 2)), dma((2, 2, steps, 2)),
            dma((2, steps, 2)), dma((2, steps, 2)),
            dma((2,)), dma((2,)), dma((2,)), dma((2,)), dma((2,)), dma((2,)),
            dma((2,)), dma((2,)), dma((2,)), dma((2,)),
        ],
        compiler_params=pltpu.CompilerParams(
            collective_id=0, has_side_effects=True, vmem_limit_bytes=56 * 1024 * 1024
        ),
    )(
        table, served_rows.reshape(1, -1), lookup_slots[0].T, block_users, w_in, w_out, out_grad[0],
    )
    return layer_out[None], table_grad.astype(F32)


def solution(mesh):
    placed = (
        P("emb", None),
        P("emb", "bal", "rep", None),
        P(),
        P(),
        P(("emb", "rep"), "bal", None),
        P(("emb", "rep"), None),
        P(("emb", "rep"), "bal", None),
    )
    return jax.shard_map(
        per_device,
        mesh=mesh,
        in_specs=placed,
        out_specs=(P(("emb", "rep"), "bal", None), P("emb", None)),
        check_vma=False,
    )
```

```python
import functools
import math

import jax
import jax.numpy as jnp
from jax import lax
from jax.experimental import pallas as pl
from jax.experimental.pallas import tpu as pltpu
from jax.sharding import PartitionSpec as P

HEADS = 4
EPS = 1e-05
MESH = pl.DeviceIdType.MESH
F32 = jnp.float32
BF16 = jnp.bfloat16


def dot(a, b):
    return jnp.dot(a, b, preferred_element_type=F32)


def dot_nt(a, b):
    return lax.dot_general(a, b, (((1,), (1,)), ((), ())), preferred_element_type=F32)


def dot_tn(a, b):
    return lax.dot_general(a, b, (((0,), (0,)), ((), ())), preferred_element_type=F32)


def sigmoid(v):
    return 0.5 * jnp.tanh(0.5 * v) + 0.5


def silu(v):
    return v * sigmoid(v)


def silu_and_slope(v):
    s = sigmoid(v)
    y = v * s
    return y, s + y * (1.0 - s)


def row_mean(v):
    return jnp.mean(v, axis=-1, keepdims=True)


def layer_kernel(
    sizes,
    table_hbm, served_hbm, lookup_hbm, users_ref, w_in_hbm, w_out_hbm, grad_hbm,
    layer_ref, tgrad_ref,
    table, served, lookup, w_in, w_out, grad, zout, zin, zback, zret, onehot, look,
    events, normed, inv_in, act, slope, nrm, datt, kv, qall,
    wt, gt, gq, att, dq, dk, dv, d_mixed, normed_att, dn, gsend, cbuf, hsend, rsbuf, agbuf,
    load_sem, a1_send, a1_recv, x1_send, x1_recv, x2_send, x2_recv,
    a2_send, a2_recv, core_send, core_recv, rs_send, rs_recv, ag_send, ag_recv,
    fan_send, fan_recv,
):
    n_emb, n_bal, n_rep = sizes
    tok, width = grad.shape
    half = width // 2
    slab = zout.shape[0] // n_emb
    cap = slab // 2
    trows = table.shape[0]
    slots = n_emb * cap
    hd = width // HEADS
    inv_root = 1.0 / math.sqrt(hd)
    e = lax.axis_index("emb")
    b = lax.axis_index("bal")
    rep = lax.axis_index("rep")
    share = gsend.shape[0] // n_rep
    part = share // n_bal

    loads = [
        pltpu.make_async_copy(src, dst, load_sem.at[i])
        for i, (src, dst) in enumerate(
            (
                (served_hbm, served), (table_hbm, table), (lookup_hbm, lookup),
                (grad_hbm, grad), (w_out_hbm, w_out), (w_in_hbm, w_in),
            )
        )
    ]
    for load in loads:
        load.start()

    barrier = pltpu.get_barrier_semaphore()

    @pl.loop(1, n_emb)
    def _(k):
        pl.semaphore_signal(
            barrier, inc=1, device_id={"emb": lax.rem(e + k, n_emb)}, device_id_type=MESH
        )

    @pl.loop(1, n_bal)
    def _(k):
        pl.semaphore_signal(
            barrier, inc=1, device_id={"bal": lax.rem(b + k, n_bal)}, device_id_type=MESH
        )

    if n_rep == 2:
        pl.semaphore_signal(barrier, inc=1, device_id={"rep": 1 - rep}, device_id_type=MESH)

    def to_slabs(both):
        halves = [
            both[:, cols].reshape(n_emb, 1, cap, half)
            for cols in (slice(0, half), slice(half, width))
        ]
        return jnp.concatenate(halves, axis=1).reshape(2 * slots, half).astype(BF16)

    def from_slabs(slabs):
        apart = slabs.astype(F32).reshape(n_emb, 2, cap, half)
        return jnp.concatenate(
            [apart[:, h].reshape(slots, half) for h in range(2)], axis=1
        ).astype(BF16)

    loads[0].wait()
    rows_of = lax.broadcasted_iota(jnp.int32, onehot.shape, 0)
    onehot[...] = jnp.where(rows_of == served[...], 1.0, 0.0).astype(BF16)
    loads[1].wait()
    zout[...] = to_slabs(dot_tn(onehot[...], table[...]))

    pl.semaphore_wait(barrier, n_emb + n_bal + n_rep - 3)

    stride = 27 if n_emb % 3 else 1

    def exchange(src, dst, send, recv):
        own = pl.ds(pl.multiple_of(e * slab, slab), slab)

        @pl.loop(1, n_emb)
        def _(k):
            to = lax.rem(e + stride * k, n_emb)
            pltpu.make_async_remote_copy(
                src_ref=src.at[pl.ds(pl.multiple_of(to * slab, slab), slab)],
                dst_ref=dst.at[own],
                send_sem=send,
                recv_sem=recv,
                device_id={"emb": to},
                device_id_type=MESH,
            ).start()

        dst[own, :] = src[own, :]
        many = pl.ds(0, (n_emb - 1) * slab)
        return pltpu.make_async_remote_copy(
            src_ref=src.at[many],
            dst_ref=dst.at[many],
            send_sem=send,
            recv_sem=recv,
            device_id={"emb": lax.rem(e + 1, n_emb)},
            device_id_type=MESH,
        )

    first = exchange(zout, zin, a1_send, a1_recv)

    loads[2].wait()
    slot_of = lax.broadcasted_iota(jnp.int32, look.shape, 0)
    hit = (slot_of == lookup[0:1, :]) | (slot_of == lookup[1:2, :])
    look[...] = jnp.where(hit, 1.0, 0.0).astype(BF16)

    my_user = users_ref[0, b]
    count = jnp.int32(0)
    for k in range(n_bal):
        count = count + jnp.where(users_ref[0, k] == my_user, 1, 0)
    inv_len = jnp.float32(0.0)
    for k in range(1, n_bal + 1):
        inv_len = jnp.where(count == k, jnp.float32(1.0 / (k * tok)), inv_len)

    for load in loads[3:]:
        load.wait()
    d_mixed[...] = dot_nt(grad[...], w_out[...])

    first.wait_recv()
    ev = dot_tn(look[...], from_slabs(zin[...]))
    events[...] = ev
    centered = ev - row_mean(ev)
    inv = lax.rsqrt(row_mean(centered * centered) + EPS)
    inv_in[...] = jnp.broadcast_to(inv, inv_in.shape)
    normed[...] = centered * inv
    nrm[0] = normed[...].astype(BF16)

    rows = tok // 4
    steps = n_bal // 2
    right = lax.rem(b + 1, n_bal)
    left = lax.rem(b + n_bal - 1, n_bal)

    def hop(buf, send, recv, way, step, c):
        if way == 0:
            src, dst, to = lax.rem(n_bal - step, n_bal), n_bal - 1 - step, right
        else:
            src, dst, to = step, step + 1, left
        piece = pl.ds(pl.multiple_of(c * rows, rows), rows)
        return pltpu.make_async_remote_copy(
            src_ref=buf.at[src, piece],
            dst_ref=buf.at[dst, piece],
            send_sem=send.at[way, step, c],
            recv_sem=recv.at[way, step, c],
            device_id={"bal": to},
            device_id_type=MESH,
        )

    def last_step(way, c):
        return jnp.where(lax.div(c, 2) == way, steps - 1, steps - 2)

    def used(causal, way, step, origin):
        if not causal:
            return step >= 0
        return origin >= steps if way == 0 else origin > step

    def sent(causal, way, step, c):
        origin = lax.rem(b + (n_bal - step if way == 0 else step), n_bal)
        return (step <= last_step(way, c)) & used(causal, way, step, origin)

    def received(causal, way, step, c):
        origin = lax.rem(b + (n_bal - 1 - step if way == 0 else step + 1), n_bal)
        return (step <= last_step(way, c)) & used(causal, way, step, origin)

    def ring_start(buf, send, recv, causal):
        @pl.loop(0, 4)
        def _(c):
            for way in range(2):
                @pl.when(sent(causal, way, 0, c))
                def _():
                    hop(buf, send, recv, way, 0, c).start()

    def ring_rest(buf, send, recv, causal, own_head, on_block):
        @pl.loop(0, steps + 1)
        def _(step):
            @pl.loop(0, 4)
            def _(c):
                for way in range(2):
                    @pl.when(received(causal, way, step, c))
                    def _():
                        hop(buf, send, recv, way, step, c).wait_recv()

                    @pl.when(sent(causal, way, step + 1, c))
                    def _():
                        hop(buf, send, recv, way, step + 1, c).start()

                @pl.when(step == 0)
                def _():
                    own_head(c)

                @pl.when((step > 0) & ((c == 1) | ((c == 3) & (step < steps))))
                def _():
                    on_block(jnp.where(c == 1, n_bal - step, step))

    def ring_drain(buf, send, recv, causal):
        @pl.loop(0, steps)
        def _(step):
            @pl.loop(0, 4)
            def _(c):
                for way in range(2):
                    @pl.when(sent(causal, way, step, c))
                    def _():
                        hop(buf, send, recv, way, step, c).wait_send()

    v_at, q_at, k_at = width, 2 * width, 3 * width

    def head(h, base=0):
        if isinstance(h, int):
            return slice(base + h * hd, base + (h + 1) * hd)
        return pl.ds(pl.multiple_of(base + h * hd, hd), hd)

    def project(*columns):
        for base in columns:
            cols = slice(base, base + width)
            a, s = silu_and_slope(dot(nrm[0], w_in[:, cols]))
            act[:, cols] = a.astype(BF16)
            slope[:, cols] = s

    def own_pair(h):
        tri_row = lax.broadcasted_iota(jnp.int32, (tok, tok), 0)
        tri_col = lax.broadcasted_iota(jnp.int32, (tok, tok), 1)
        q, k, v = act[:, head(h, q_at)], act[:, head(h, k_at)], act[:, head(h, v_at)]
        y, g = silu_and_slope(dot_nt(q, k) * inv_root)
        keep = tri_row >= tri_col
        att[:, head(h)] = dot(jnp.where(keep, y * inv_len, 0.0).astype(BF16), v)
        gq[0, h] = jnp.where(keep, g * inv_len, 0.0)
        y, g = silu_and_slope(dot_nt(k, q) * inv_root)
        keep = tri_row <= tri_col
        wt[0, h] = jnp.where(keep, y * inv_len, 0.0).astype(BF16)
        gt[0, h] = jnp.where(keep, g * inv_len, 0.0)

    ring_start(nrm, x1_send, x1_recv, False)
    project(q_at, k_at, v_at, 0)

    def seen(j):
        return jnp.where(users_ref[0, j] == my_user, inv_len, jnp.float32(0.0))

    def forward_block(r):
        j = lax.rem(b + r, n_bal)
        f = seen(j)

        @pl.when(j < b)
        def _():
            x = nrm[r]
            kv[r, :, :width] = silu(dot(x, w_in[:, v_at : v_at + width])).astype(BF16)
            kv[r, :, width:] = silu(dot(x, w_in[:, k_at : k_at + width])).astype(BF16)
            for h in range(HEADS):
                k = kv[r, :, head(h, width)]
                y, g = silu_and_slope(dot_nt(act[:, head(h, q_at)], k) * inv_root)
                gq[r, h] = g * f
                att[:, head(h)] += dot((y * f).astype(BF16), kv[r, :, head(h)])

        @pl.when(j > b)
        def _():
            qall[r] = silu(dot(nrm[r], w_in[:, q_at : q_at + width])).astype(BF16)
            for h in range(HEADS):
                y, g = silu_and_slope(
                    dot_nt(act[:, head(h, k_at)], qall[r, :, head(h)]) * inv_root
                )
                gt[r, h] = g * f
                wt[r, h] = (y * f).astype(BF16)

    ring_rest(nrm, x1_send, x1_recv, False, own_pair, forward_block)

    at = att[...]
    centered = at - row_mean(at)
    inv_att = lax.rsqrt(row_mean(centered * centered) + EPS)
    na = centered * inv_att
    normed_att[...] = na
    d_gated = d_mixed[...] * act[:, :width].astype(F32)
    d_att = (
        (d_gated - row_mean(d_gated) - na * row_mean(d_gated * na)) * inv_att
    ).astype(BF16)
    datt[0] = d_att

    def own_pair_back(h):
        q, k, v = act[:, head(h, q_at)], act[:, head(h, k_at)], act[:, head(h, v_at)]
        d = datt[0, :, head(h)]
        ds = (dot_nt(d, v) * gq[0, h]).astype(BF16)
        dq[:, head(h)] = dot(ds, k)
        dv[:, head(h)] = dot(wt[0, h], d)
        dst = (dot_nt(v, d) * gt[0, h]).astype(BF16)
        dk[:, head(h)] = dot(dst, q)

    def own_layer():
        mixed = (normed_att[...] * act[:, :width].astype(F32)).astype(BF16)
        layer_ref[...] = (events[...] + dot(mixed, w_out[...])).astype(BF16)

    def own_gate():
        d_pre = (d_mixed[...] * normed_att[...] * slope[:, :width]).astype(BF16)
        dn[...] = dot_nt(d_pre, w_in[:, :width])

    ring_start(datt, x2_send, x2_recv, True)
    own_layer()
    own_gate()

    def backward_block(r):
        j = lax.rem(b + r, n_bal)

        @pl.when(j < b)
        def _():
            for h in range(HEADS):
                ds = (dot_nt(datt[0, :, head(h)], kv[r, :, head(h)]) * gq[r, h]).astype(BF16)
                dq[:, head(h)] += dot(ds, kv[r, :, head(h, width)])

        @pl.when(j > b)
        def _():
            for h in range(HEADS):
                d = datt[r, :, head(h)]
                dv[:, head(h)] += dot(wt[r, h], d)
                dst = (dot_nt(act[:, head(h, v_at)], d) * gt[r, h]).astype(BF16)
                dk[:, head(h)] += dot(dst, qall[r, :, head(h)])

    ring_rest(datt, x2_send, x2_recv, True, own_pair_back, backward_block)

    d_normed = dn[...]
    for base, acc, scale in ((v_at, dv, 1.0), (q_at, dq, inv_root), (k_at, dk, inv_root)):
        d_pre = (acc[...] * scale * slope[:, base : base + width]).astype(BF16)
        d_normed = d_normed + dot_nt(d_pre, w_in[:, base : base + width])
    nr = normed[...]
    d_events = (
        grad[...].astype(F32)
        + (d_normed - row_mean(d_normed) - nr * row_mean(d_normed * nr)) * inv_in[:, 0:1]
    ).astype(BF16)

    zback[...] = to_slabs(dot(look[...], d_events))
    second = exchange(zback, zret, a2_send, a2_recv)
    first.wait_send()
    ring_drain(nrm, x1_send, x1_recv, False)
    ring_drain(datt, x2_send, x2_recv, True)
    second.wait_recv()
    grads = dot(onehot[...], from_slabs(zret[...])).astype(BF16)
    gsend[:trows, :] = grads[:, :half]
    gsend[trows:, :] = grads[:, half:]

    ours = pl.ds(pl.multiple_of(rep * share, share), share)
    own_part = pl.ds(pl.multiple_of(b * part, part), part)
    if n_rep == 2:
        theirs = pl.ds(pl.multiple_of((1 - rep) * share, share), share)
        swap = pltpu.make_async_remote_copy(
            src_ref=gsend.at[theirs], dst_ref=cbuf, send_sem=core_send, recv_sem=core_recv,
            device_id={"rep": 1 - rep}, device_id_type=MESH,
        )
        swap.start()
        swap.wait_recv()
        hsend[...] = (gsend[ours, :].astype(F32) + cbuf[...].astype(F32)).astype(BF16)
    else:
        hsend[...] = gsend[...]

    @pl.loop(1, n_bal)
    def _(k):
        c = lax.rem(b + k, n_bal)
        pltpu.make_async_remote_copy(
            src_ref=hsend.at[pl.ds(pl.multiple_of(c * part, part), part)],
            dst_ref=rsbuf.at[own_part],
            send_sem=rs_send,
            recv_sem=rs_recv,
            device_id={"bal": c},
            device_id_type=MESH,
        ).start()

    rsbuf[own_part, :] = hsend[own_part, :]
    others = pl.ds(0, (n_bal - 1) * part)
    reduced = pltpu.make_async_remote_copy(
        src_ref=hsend.at[others], dst_ref=rsbuf.at[others],
        send_sem=rs_send, recv_sem=rs_recv, device_id={"bal": right}, device_id_type=MESH,
    )
    second.wait_send()
    reduced.wait_recv()
    total = rsbuf[0:part, :].astype(F32)
    for k in range(1, n_bal):
        total = total + rsbuf[k * part : (k + 1) * part, :].astype(F32)
    mine_at = pl.ds(pl.multiple_of(rep * share + b * part, part), part)
    agbuf[mine_at, :] = total.astype(BF16)

    @pl.loop(1, n_bal)
    def _(k):
        pltpu.make_async_remote_copy(
            src_ref=agbuf.at[mine_at],
            dst_ref=agbuf.at[mine_at],
            send_sem=ag_send,
            recv_sem=ag_recv,
            device_id={"bal": lax.rem(b + k, n_bal)},
            device_id_type=MESH,
        ).start()

    gathered = pltpu.make_async_remote_copy(
        src_ref=agbuf.at[others], dst_ref=agbuf.at[others],
        send_sem=ag_send, recv_sem=ag_recv, device_id={"bal": right}, device_id_type=MESH,
    )
    reduced.wait_send()
    gathered.wait_recv()
    if n_rep == 2:
        fan = pltpu.make_async_remote_copy(
            src_ref=agbuf.at[ours], dst_ref=agbuf.at[ours], send_sem=fan_send,
            recv_sem=fan_recv, device_id={"rep": 1 - rep}, device_id_type=MESH,
        )
        fan.start()
        swap.wait_send()
        fan.wait_recv()
    tgrad_ref[:, :half] = agbuf[:trows, :]
    tgrad_ref[:, half:] = agbuf[trows:, :]
    gathered.wait_send()
    if n_rep == 2:
        fan.wait_send()


def per_device(table, served_rows, w_in, w_out, lookup_slots, block_users, out_grad):
    n_emb, n_bal, n_rep = (lax.axis_size(a) for a in ("emb", "bal", "rep"))
    trows, width = table.shape
    tok = lookup_slots.shape[1]
    half = width // 2
    steps = n_bal // 2
    slots = 2 * served_rows.shape[-1]
    hd = width // HEADS
    vmem = pl.BlockSpec(memory_space=pltpu.VMEM)
    hbm = pl.BlockSpec(memory_space=pltpu.HBM)
    dma = pltpu.SemaphoreType.DMA
    share = 2 * trows // n_rep
    layer_out, table_grad = pl.pallas_call(
        functools.partial(layer_kernel, (n_emb, n_bal, n_rep)),
        out_shape=(
            pltpu.VMEM((tok, width), BF16),
            pltpu.VMEM((trows, width), BF16),
        ),
        in_specs=[hbm, hbm, hbm, pl.BlockSpec(memory_space=pltpu.SMEM), hbm, hbm, hbm],
        out_specs=(vmem, vmem),
        scratch_shapes=[
            pltpu.VMEM((trows, width), BF16),
            pltpu.VMEM((1, slots // 2), jnp.int32),
            pltpu.VMEM((2, tok), jnp.int32),
            pltpu.VMEM((width, 4 * width), BF16),
            pltpu.VMEM((width, width), BF16),
            pltpu.VMEM((tok, width), BF16),
            pltpu.VMEM((slots, half), BF16),
            pltpu.VMEM((slots, half), BF16),
            pltpu.VMEM((slots, half), BF16),
            pltpu.VMEM((slots, half), BF16),
            pltpu.VMEM((trows, slots // 2), BF16),
            pltpu.VMEM((slots // 2, tok), BF16),
            pltpu.VMEM((tok, width), F32),
            pltpu.VMEM((tok, width), F32),
            pltpu.VMEM((tok, 128), F32),
            pltpu.VMEM((tok, 4 * width), BF16),
            pltpu.VMEM((tok, 4 * width), F32),
            pltpu.VMEM((n_bal, tok, width), BF16),
            pltpu.VMEM((n_bal, tok, width), BF16),
            pltpu.VMEM((n_bal, tok, 2 * width), BF16),
            pltpu.VMEM((n_bal, tok, width), BF16),
            pltpu.VMEM((n_bal, HEADS, tok, tok), BF16),
            pltpu.VMEM((n_bal, HEADS, tok, tok), F32),
            pltpu.VMEM((n_bal, HEADS, tok, tok), F32),
            pltpu.VMEM((tok, width), F32),
            pltpu.VMEM((tok, width), F32),
            pltpu.VMEM((tok, width), F32),
            pltpu.VMEM((tok, width), F32),
            pltpu.VMEM((tok, width), F32),
            pltpu.VMEM((tok, width), F32),
            pltpu.VMEM((tok, width), F32),
            pltpu.VMEM((2 * trows, half), BF16),
            pltpu.VMEM((share, half), BF16),
            pltpu.VMEM((share, half), BF16),
            pltpu.VMEM((share, half), BF16),
            pltpu.VMEM((2 * trows, half), BF16),
            dma((6,)),
            dma, dma,
            dma((2, steps, 4)), dma((2, steps, 4)),
            dma((2, steps, 4)), dma((2, steps, 4)),
            dma, dma, dma, dma, dma, dma, dma, dma, dma, dma,
        ],
        compiler_params=pltpu.CompilerParams(
            collective_id=0, has_side_effects=True, vmem_limit_bytes=56 * 1024 * 1024
        ),
    )(
        table, served_rows.reshape(1, -1), lookup_slots[0].T, block_users, w_in, w_out, out_grad[0],
    )
    return layer_out[None], table_grad.astype(F32)


def solution(mesh):
    placed = (
        P("emb", None),
        P("emb", "bal", "rep", None),
        P(),
        P(),
        P(("emb", "rep"), "bal", None),
        P(("emb", "rep"), None),
        P(("emb", "rep"), "bal", None),
    )
    return jax.shard_map(
        per_device,
        mesh=mesh,
        in_specs=placed,
        out_specs=(P(("emb", "rep"), "bal", None), P("emb", None)),
        check_vma=False,
    )
```

```python
import functools
import math

import jax
import jax.numpy as jnp
from jax import lax
from jax.experimental import pallas as pl
from jax.experimental.pallas import tpu as pltpu
from jax.sharding import PartitionSpec as P

HEADS = 4
EPS = 1e-05
MESH = pl.DeviceIdType.MESH
F32 = jnp.float32
BF16 = jnp.bfloat16


def dot(a, b):
    return jnp.dot(a, b, preferred_element_type=F32)


def dot_nt(a, b):
    return lax.dot_general(a, b, (((1,), (1,)), ((), ())), preferred_element_type=F32)


def dot_tn(a, b):
    return lax.dot_general(a, b, (((0,), (0,)), ((), ())), preferred_element_type=F32)


def sigmoid(v):
    return 0.5 * jnp.tanh(0.5 * v) + 0.5


def silu(v):
    return v * sigmoid(v)


def silu_and_slope(v):
    s = sigmoid(v)
    y = v * s
    return y, s + y * (1.0 - s)


def row_mean(v):
    return jnp.mean(v, axis=-1, keepdims=True)


def layer_kernel(
    sizes,
    table_hbm, served_hbm, lookup_hbm, users_ref, w_in_hbm, w_out_hbm, grad_hbm,
    layer_ref, tgrad_ref,
    table, served, lookup, w_in, w_out, grad, zout, zin, zback, zret, onehot, look,
    events, normed, inv_in, act, slope, nrm, datt, kv, qall,
    wt, gt, gq, att, dq, dk, dv, d_mixed, normed_att, dn, gsend, cbuf, hsend, rsbuf, agbuf,
    load_sem, a1_send, a1_recv, x1_send, x1_recv, x2_send, x2_recv,
    a2_send, a2_recv, core_send, core_recv, rs_send, rs_recv, ag_send, ag_recv,
    fan_send, fan_recv,
):
    n_emb, n_bal, n_rep = sizes
    tok, width = grad.shape
    half = width // 2
    slab = zout.shape[0] // n_emb
    cap = slab // 2
    trows = table.shape[0]
    slots = n_emb * cap
    hd = width // HEADS
    inv_root = 1.0 / math.sqrt(hd)
    e = lax.axis_index("emb")
    b = lax.axis_index("bal")
    rep = lax.axis_index("rep")
    share = trows // n_rep
    part = share // n_bal

    loads = [
        pltpu.make_async_copy(src, dst, load_sem.at[i])
        for i, (src, dst) in enumerate(
            (
                (served_hbm, served), (table_hbm, table), (lookup_hbm, lookup),
                (grad_hbm, grad), (w_out_hbm, w_out), (w_in_hbm, w_in),
            )
        )
    ]
    for load in loads:
        load.start()

    barrier = pltpu.get_barrier_semaphore()

    @pl.loop(1, n_emb)
    def _(k):
        pl.semaphore_signal(
            barrier, inc=1, device_id={"emb": lax.rem(e + k, n_emb)}, device_id_type=MESH
        )

    @pl.loop(1, n_bal)
    def _(k):
        pl.semaphore_signal(
            barrier, inc=1, device_id={"bal": lax.rem(b + k, n_bal)}, device_id_type=MESH
        )

    if n_rep == 2:
        pl.semaphore_signal(barrier, inc=1, device_id={"rep": 1 - rep}, device_id_type=MESH)

    def to_slabs(both):
        halves = [
            both[:, cols].reshape(n_emb, 1, cap, half)
            for cols in (slice(0, half), slice(half, width))
        ]
        return jnp.concatenate(halves, axis=1).reshape(2 * slots, half).astype(BF16)

    def from_slabs(slabs):
        apart = slabs.astype(F32).reshape(n_emb, 2, cap, half)
        return jnp.concatenate(
            [apart[:, h].reshape(slots, half) for h in range(2)], axis=1
        ).astype(BF16)

    loads[0].wait()
    rows_of = lax.broadcasted_iota(jnp.int32, onehot.shape, 0)
    onehot[...] = jnp.where(rows_of == served[...], 1.0, 0.0).astype(BF16)
    loads[1].wait()
    zout[...] = to_slabs(dot_tn(onehot[...], table[...]))

    pl.semaphore_wait(barrier, n_emb + n_bal + n_rep - 3)

    stride = 27 if n_emb % 3 else 1

    def exchange(src, dst, send, recv):
        own = pl.ds(pl.multiple_of(e * slab, slab), slab)

        @pl.loop(1, n_emb)
        def _(k):
            to = lax.rem(e + stride * k, n_emb)
            pltpu.make_async_remote_copy(
                src_ref=src.at[pl.ds(pl.multiple_of(to * slab, slab), slab)],
                dst_ref=dst.at[own],
                send_sem=send,
                recv_sem=recv,
                device_id={"emb": to},
                device_id_type=MESH,
            ).start()

        dst[own, :] = src[own, :]
        many = pl.ds(0, (n_emb - 1) * slab)
        return pltpu.make_async_remote_copy(
            src_ref=src.at[many],
            dst_ref=dst.at[many],
            send_sem=send,
            recv_sem=recv,
            device_id={"emb": lax.rem(e + 1, n_emb)},
            device_id_type=MESH,
        )

    first = exchange(zout, zin, a1_send, a1_recv)

    loads[2].wait()
    slot_of = lax.broadcasted_iota(jnp.int32, look.shape, 0)
    hit = (slot_of == lookup[0:1, :]) | (slot_of == lookup[1:2, :])
    look[...] = jnp.where(hit, 1.0, 0.0).astype(BF16)

    my_user = users_ref[0, b]
    count = jnp.int32(0)
    for k in range(n_bal):
        count = count + jnp.where(users_ref[0, k] == my_user, 1, 0)
    inv_len = jnp.float32(0.0)
    for k in range(1, n_bal + 1):
        inv_len = jnp.where(count == k, jnp.float32(1.0 / (k * tok)), inv_len)

    for load in loads[3:]:
        load.wait()
    d_mixed[...] = dot_nt(grad[...], w_out[...])

    first.wait_recv()
    ev = dot_tn(look[...], from_slabs(zin[...]))
    events[...] = ev
    centered = ev - row_mean(ev)
    inv = lax.rsqrt(row_mean(centered * centered) + EPS)
    inv_in[...] = jnp.broadcast_to(inv, inv_in.shape)
    normed[...] = centered * inv
    nrm[0] = normed[...].astype(BF16)

    rows = tok // 4
    steps = n_bal // 2
    right = lax.rem(b + 1, n_bal)
    left = lax.rem(b + n_bal - 1, n_bal)

    def hop(buf, send, recv, way, step, c):
        if way == 0:
            src, dst, to = lax.rem(n_bal - step, n_bal), n_bal - 1 - step, right
        else:
            src, dst, to = step, step + 1, left
        piece = pl.ds(pl.multiple_of(c * rows, rows), rows)
        return pltpu.make_async_remote_copy(
            src_ref=buf.at[src, piece],
            dst_ref=buf.at[dst, piece],
            send_sem=send.at[way, step, c],
            recv_sem=recv.at[way, step, c],
            device_id={"bal": to},
            device_id_type=MESH,
        )

    def last_step(way, c):
        return jnp.where(lax.div(c, 2) == way, steps - 1, steps - 2)

    def used(causal, way, step, origin):
        if not causal:
            return step >= 0
        return origin >= steps if way == 0 else origin > step

    def sent(causal, way, step, c):
        origin = lax.rem(b + (n_bal - step if way == 0 else step), n_bal)
        return (step <= last_step(way, c)) & used(causal, way, step, origin)

    def received(causal, way, step, c):
        origin = lax.rem(b + (n_bal - 1 - step if way == 0 else step + 1), n_bal)
        return (step <= last_step(way, c)) & used(causal, way, step, origin)

    def ring_start(buf, send, recv, causal):
        @pl.loop(0, 4)
        def _(c):
            for way in range(2):
                @pl.when(sent(causal, way, 0, c))
                def _():
                    hop(buf, send, recv, way, 0, c).start()

    def ring_rest(buf, send, recv, causal, own_head, on_block):
        @pl.loop(0, steps + 1)
        def _(step):
            @pl.loop(0, 4)
            def _(c):
                for way in range(2):
                    @pl.when(received(causal, way, step, c))
                    def _():
                        hop(buf, send, recv, way, step, c).wait_recv()

                    @pl.when(sent(causal, way, step + 1, c))
                    def _():
                        hop(buf, send, recv, way, step + 1, c).start()

                @pl.when(step == 0)
                def _():
                    own_head(c)

                @pl.when((step > 0) & ((c == 1) | ((c == 3) & (step < steps))))
                def _():
                    on_block(jnp.where(c == 1, n_bal - step, step))

    def ring_drain(buf, send, recv, causal):
        @pl.loop(0, steps)
        def _(step):
            @pl.loop(0, 4)
            def _(c):
                for way in range(2):
                    @pl.when(sent(causal, way, step, c))
                    def _():
                        hop(buf, send, recv, way, step, c).wait_send()

    v_at, q_at, k_at = width, 2 * width, 3 * width

    def head(h, base=0):
        if isinstance(h, int):
            return slice(base + h * hd, base + (h + 1) * hd)
        return pl.ds(pl.multiple_of(base + h * hd, hd), hd)

    def project(*columns):
        for base in columns:
            cols = slice(base, base + width)
            a, s = silu_and_slope(dot(nrm[0], w_in[:, cols]))
            act[:, cols] = a.astype(BF16)
            slope[:, cols] = s

    def own_pair(h):
        tri_row = lax.broadcasted_iota(jnp.int32, (tok, tok), 0)
        tri_col = lax.broadcasted_iota(jnp.int32, (tok, tok), 1)
        q, k, v = act[:, head(h, q_at)], act[:, head(h, k_at)], act[:, head(h, v_at)]
        y, g = silu_and_slope(dot_nt(q, k) * inv_root)
        keep = tri_row >= tri_col
        att[:, head(h)] = dot(jnp.where(keep, y * inv_len, 0.0).astype(BF16), v)
        gq[0, h] = jnp.where(keep, g * inv_len, 0.0)
        y, g = silu_and_slope(dot_nt(k, q) * inv_root)
        keep = tri_row <= tri_col
        wt[0, h] = jnp.where(keep, y * inv_len, 0.0).astype(BF16)
        gt[0, h] = jnp.where(keep, g * inv_len, 0.0)

    ring_start(nrm, x1_send, x1_recv, False)
    project(q_at, k_at, v_at, 0)

    def seen(j):
        return jnp.where(users_ref[0, j] == my_user, inv_len, jnp.float32(0.0))

    def forward_block(r):
        j = lax.rem(b + r, n_bal)
        f = seen(j)

        @pl.when(j < b)
        def _():
            x = nrm[r]
            kv[r, :, :width] = silu(dot(x, w_in[:, v_at : v_at + width])).astype(BF16)
            kv[r, :, width:] = silu(dot(x, w_in[:, k_at : k_at + width])).astype(BF16)
            for h in range(HEADS):
                k = kv[r, :, head(h, width)]
                y, g = silu_and_slope(dot_nt(act[:, head(h, q_at)], k) * inv_root)
                gq[r, h] = g * f
                att[:, head(h)] += dot((y * f).astype(BF16), kv[r, :, head(h)])

        @pl.when(j > b)
        def _():
            qall[r] = silu(dot(nrm[r], w_in[:, q_at : q_at + width])).astype(BF16)
            for h in range(HEADS):
                y, g = silu_and_slope(
                    dot_nt(act[:, head(h, k_at)], qall[r, :, head(h)]) * inv_root
                )
                gt[r, h] = g * f
                wt[r, h] = (y * f).astype(BF16)

    ring_rest(nrm, x1_send, x1_recv, False, own_pair, forward_block)

    at = att[...]
    centered = at - row_mean(at)
    inv_att = lax.rsqrt(row_mean(centered * centered) + EPS)
    na = centered * inv_att
    normed_att[...] = na
    d_gated = d_mixed[...] * act[:, :width].astype(F32)
    d_att = (
        (d_gated - row_mean(d_gated) - na * row_mean(d_gated * na)) * inv_att
    ).astype(BF16)
    datt[0] = d_att

    def own_pair_back(h):
        q, k, v = act[:, head(h, q_at)], act[:, head(h, k_at)], act[:, head(h, v_at)]
        d = datt[0, :, head(h)]
        ds = (dot_nt(d, v) * gq[0, h]).astype(BF16)
        dq[:, head(h)] = dot(ds, k)
        dv[:, head(h)] = dot(wt[0, h], d)
        dst = (dot_nt(v, d) * gt[0, h]).astype(BF16)
        dk[:, head(h)] = dot(dst, q)

    def own_layer():
        mixed = (normed_att[...] * act[:, :width].astype(F32)).astype(BF16)
        layer_ref[...] = (events[...] + dot(mixed, w_out[...])).astype(BF16)

    def own_gate():
        d_pre = (d_mixed[...] * normed_att[...] * slope[:, :width]).astype(BF16)
        dn[...] = dot_nt(d_pre, w_in[:, :width])

    ring_start(datt, x2_send, x2_recv, True)
    own_layer()
    own_gate()

    def backward_block(r):
        j = lax.rem(b + r, n_bal)

        @pl.when(j < b)
        def _():
            for h in range(HEADS):
                ds = (dot_nt(datt[0, :, head(h)], kv[r, :, head(h)]) * gq[r, h]).astype(BF16)
                dq[:, head(h)] += dot(ds, kv[r, :, head(h, width)])

        @pl.when(j > b)
        def _():
            for h in range(HEADS):
                d = datt[r, :, head(h)]
                dv[:, head(h)] += dot(wt[r, h], d)
                dst = (dot_nt(act[:, head(h, v_at)], d) * gt[r, h]).astype(BF16)
                dk[:, head(h)] += dot(dst, qall[r, :, head(h)])

    ring_rest(datt, x2_send, x2_recv, True, own_pair_back, backward_block)

    d_normed = dn[...]
    for base, acc, scale in ((v_at, dv, 1.0), (q_at, dq, inv_root), (k_at, dk, inv_root)):
        d_pre = (acc[...] * scale * slope[:, base : base + width]).astype(BF16)
        d_normed = d_normed + dot_nt(d_pre, w_in[:, base : base + width])
    nr = normed[...]
    d_events = (
        grad[...].astype(F32)
        + (d_normed - row_mean(d_normed) - nr * row_mean(d_normed * nr)) * inv_in[:, 0:1]
    ).astype(BF16)

    zback[...] = to_slabs(dot(look[...], d_events))
    second = exchange(zback, zret, a2_send, a2_recv)
    first.wait_send()
    ring_drain(nrm, x1_send, x1_recv, False)
    ring_drain(datt, x2_send, x2_recv, True)
    second.wait_recv()

    ours = pl.ds(pl.multiple_of(rep * share, share), share)
    theirs = pl.ds(pl.multiple_of((n_rep - 1 - rep) * share, share), share)
    own_part = pl.ds(pl.multiple_of(b * part, part), part)
    mine_at = pl.ds(pl.multiple_of(rep * share + b * part, part), part)
    others = pl.ds(0, (n_bal - 1) * part)
    other_core = {"rep": n_rep - 1 - rep}

    def remote(src, dst, send, recv, where):
        return pltpu.make_async_remote_copy(
            src_ref=src, dst_ref=dst, send_sem=send, recv_sem=recv,
            device_id=where, device_id_type=MESH,
        )

    both = range(2)
    swaps = [
        remote(gsend.at[c, theirs], cbuf.at[c], core_send.at[c], core_recv.at[c], other_core)
        for c in both
    ]
    fans = [
        remote(agbuf.at[c, ours], agbuf.at[c, ours], fan_send.at[c], fan_recv.at[c], other_core)
        for c in both
    ]
    reduced = [
        remote(
            hsend.at[c, others], rsbuf.at[c, others], rs_send.at[c], rs_recv.at[c],
            {"bal": right},
        )
        for c in both
    ]
    gathered = [
        remote(
            agbuf.at[c, others], agbuf.at[c, others], ag_send.at[c], ag_recv.at[c],
            {"bal": right},
        )
        for c in both
    ]
    apart = zret[...].astype(F32).reshape(n_emb, 2, cap, half)
    for c in both:
        back = apart[:, c].reshape(slots, half).astype(BF16)
        gsend[c] = dot(onehot[...], back).astype(BF16)
        if n_rep == 2:
            swaps[c].start()

    for c in both:
        if n_rep == 2:
            swaps[c].wait_recv()
            hsend[c] = (gsend[c, ours, :].astype(F32) + cbuf[c].astype(F32)).astype(BF16)
        else:
            hsend[c] = gsend[c]

        @pl.loop(1, n_bal)
        def _(k):
            to = lax.rem(b + k, n_bal)
            remote(
                hsend.at[c, pl.ds(pl.multiple_of(to * part, part), part)],
                rsbuf.at[c, own_part], rs_send.at[c], rs_recv.at[c], {"bal": to},
            ).start()

        rsbuf[c, own_part, :] = hsend[c, own_part, :]

    second.wait_send()
    for c in both:
        reduced[c].wait_recv()
        total = rsbuf[c, 0:part, :].astype(F32)
        for k in range(1, n_bal):
            total = total + rsbuf[c, k * part : (k + 1) * part, :].astype(F32)
        agbuf[c, mine_at, :] = total.astype(BF16)

        @pl.loop(1, n_bal)
        def _(k):
            remote(
                agbuf.at[c, mine_at], agbuf.at[c, mine_at], ag_send.at[c], ag_recv.at[c],
                {"bal": lax.rem(b + k, n_bal)},
            ).start()

    for c in both:
        gathered[c].wait_recv()
        if n_rep == 2:
            fans[c].start()
    for c in both:
        if n_rep == 2:
            fans[c].wait_recv()
        tgrad_ref[:, c * half : (c + 1) * half] = agbuf[c]
    for c in both:
        reduced[c].wait_send()
        gathered[c].wait_send()
        if n_rep == 2:
            swaps[c].wait_send()
            fans[c].wait_send()


def per_device(table, served_rows, w_in, w_out, lookup_slots, block_users, out_grad):
    n_emb, n_bal, n_rep = (lax.axis_size(a) for a in ("emb", "bal", "rep"))
    trows, width = table.shape
    tok = lookup_slots.shape[1]
    half = width // 2
    steps = n_bal // 2
    slots = 2 * served_rows.shape[-1]
    hd = width // HEADS
    vmem = pl.BlockSpec(memory_space=pltpu.VMEM)
    hbm = pl.BlockSpec(memory_space=pltpu.HBM)
    dma = pltpu.SemaphoreType.DMA
    share = trows // n_rep
    layer_out, table_grad = pl.pallas_call(
        functools.partial(layer_kernel, (n_emb, n_bal, n_rep)),
        out_shape=(
            pltpu.VMEM((tok, width), BF16),
            pltpu.VMEM((trows, width), BF16),
        ),
        in_specs=[hbm, hbm, hbm, pl.BlockSpec(memory_space=pltpu.SMEM), hbm, hbm, hbm],
        out_specs=(vmem, vmem),
        scratch_shapes=[
            pltpu.VMEM((trows, width), BF16),
            pltpu.VMEM((1, slots // 2), jnp.int32),
            pltpu.VMEM((2, tok), jnp.int32),
            pltpu.VMEM((width, 4 * width), BF16),
            pltpu.VMEM((width, width), BF16),
            pltpu.VMEM((tok, width), BF16),
            pltpu.VMEM((slots, half), BF16),
            pltpu.VMEM((slots, half), BF16),
            pltpu.VMEM((slots, half), BF16),
            pltpu.VMEM((slots, half), BF16),
            pltpu.VMEM((trows, slots // 2), BF16),
            pltpu.VMEM((slots // 2, tok), BF16),
            pltpu.VMEM((tok, width), F32),
            pltpu.VMEM((tok, width), F32),
            pltpu.VMEM((tok, 128), F32),
            pltpu.VMEM((tok, 4 * width), BF16),
            pltpu.VMEM((tok, 4 * width), F32),
            pltpu.VMEM((n_bal, tok, width), BF16),
            pltpu.VMEM((n_bal, tok, width), BF16),
            pltpu.VMEM((n_bal, tok, 2 * width), BF16),
            pltpu.VMEM((n_bal, tok, width), BF16),
            pltpu.VMEM((n_bal, HEADS, tok, tok), BF16),
            pltpu.VMEM((n_bal, HEADS, tok, tok), F32),
            pltpu.VMEM((n_bal, HEADS, tok, tok), F32),
            pltpu.VMEM((tok, width), F32),
            pltpu.VMEM((tok, width), F32),
            pltpu.VMEM((tok, width), F32),
            pltpu.VMEM((tok, width), F32),
            pltpu.VMEM((tok, width), F32),
            pltpu.VMEM((tok, width), F32),
            pltpu.VMEM((tok, width), F32),
            pltpu.VMEM((2, trows, half), BF16),
            pltpu.VMEM((2, share, half), BF16),
            pltpu.VMEM((2, share, half), BF16),
            pltpu.VMEM((2, share, half), BF16),
            pltpu.VMEM((2, trows, half), BF16),
            dma((6,)),
            dma, dma,
            dma((2, steps, 4)), dma((2, steps, 4)),
            dma((2, steps, 4)), dma((2, steps, 4)),
            dma, dma,
            dma((2,)), dma((2,)), dma((2,)), dma((2,)),
            dma((2,)), dma((2,)), dma((2,)), dma((2,)),
        ],
        compiler_params=pltpu.CompilerParams(
            collective_id=0, has_side_effects=True, vmem_limit_bytes=56 * 1024 * 1024
        ),
    )(
        table, served_rows.reshape(1, -1), lookup_slots[0].T, block_users, w_in, w_out, out_grad[0],
    )
    return layer_out[None], table_grad.astype(F32)


def solution(mesh):
    placed = (
        P("emb", None),
        P("emb", "bal", "rep", None),
        P(),
        P(),
        P(("emb", "rep"), "bal", None),
        P(("emb", "rep"), None),
        P(("emb", "rep"), "bal", None),
    )
    return jax.shard_map(
        per_device,
        mesh=mesh,
        in_specs=placed,
        out_specs=(P(("emb", "rep"), "bal", None), P("emb", None)),
        check_vma=False,
    )
```

```python
import functools
import math

import jax
import jax.numpy as jnp
from jax import lax
from jax.experimental import pallas as pl
from jax.experimental.pallas import tpu as pltpu
from jax.sharding import PartitionSpec as P

HEADS = 4
EPS = 1e-05
MESH = pl.DeviceIdType.MESH
F32 = jnp.float32
BF16 = jnp.bfloat16


def dot(a, b):
    return jnp.dot(a, b, preferred_element_type=F32)


def dot_nt(a, b):
    return lax.dot_general(a, b, (((1,), (1,)), ((), ())), preferred_element_type=F32)


def dot_tn(a, b):
    return lax.dot_general(a, b, (((0,), (0,)), ((), ())), preferred_element_type=F32)


def sigmoid(v):
    return 0.5 * jnp.tanh(0.5 * v) + 0.5


def silu(v):
    return v * sigmoid(v)


def silu_and_slope(v):
    s = sigmoid(v)
    y = v * s
    return y, s + y * (1.0 - s)


def row_mean(v):
    return jnp.mean(v, axis=-1, keepdims=True)


def layer_kernel(
    sizes,
    table_hbm, served_hbm, lookup_hbm, users_ref, w_in_hbm, w_out_hbm, grad_hbm,
    layer_ref, tgrad_ref,
    table, served, lookup, w_in, w_out, grad, zout, zin, zback, zret, onehot, look,
    events, normed, inv_in, act, slope, nrm, datt, kv, qall,
    wt, gt, gq, att, dq, dk, dv, d_mixed, normed_att, dn, gsend, cbuf, hsend, rsbuf, agbuf,
    load_sem, a1_send, a1_recv, x1_send, x1_recv, x2_send, x2_recv,
    a2_send, a2_recv, core_send, core_recv, rs_send, rs_recv, ag_send, ag_recv,
    fan_send, fan_recv,
):
    n_emb, n_bal, n_rep = sizes
    tok, width = grad.shape
    half = width // 2
    slab = zout.shape[0] // n_emb
    cap = slab // 2
    trows = table.shape[0]
    slots = n_emb * cap
    hd = width // HEADS
    inv_root = 1.0 / math.sqrt(hd)
    e = lax.axis_index("emb")
    b = lax.axis_index("bal")
    rep = lax.axis_index("rep")
    share = trows // n_rep
    part = share // n_bal

    loads = [
        pltpu.make_async_copy(src, dst, load_sem.at[i])
        for i, (src, dst) in enumerate(
            (
                (served_hbm, served), (table_hbm, table), (lookup_hbm, lookup),
                (grad_hbm, grad), (w_out_hbm, w_out), (w_in_hbm, w_in),
            )
        )
    ]
    for load in loads:
        load.start()

    barrier = pltpu.get_barrier_semaphore()

    @pl.loop(1, n_emb)
    def _(k):
        pl.semaphore_signal(
            barrier, inc=1, device_id={"emb": lax.rem(e + k, n_emb)}, device_id_type=MESH
        )

    @pl.loop(1, n_bal)
    def _(k):
        pl.semaphore_signal(
            barrier, inc=1, device_id={"bal": lax.rem(b + k, n_bal)}, device_id_type=MESH
        )

    if n_rep == 2:
        pl.semaphore_signal(barrier, inc=1, device_id={"rep": 1 - rep}, device_id_type=MESH)

    def to_slabs(both):
        halves = [
            both[:, cols].reshape(n_emb, 1, cap, half)
            for cols in (slice(0, half), slice(half, width))
        ]
        return jnp.concatenate(halves, axis=1).reshape(2 * slots, half).astype(BF16)

    def from_slabs(slabs):
        apart = slabs.astype(F32).reshape(n_emb, 2, cap, half)
        return jnp.concatenate(
            [apart[:, h].reshape(slots, half) for h in range(2)], axis=1
        ).astype(BF16)

    loads[0].wait()
    rows_of = lax.broadcasted_iota(jnp.int32, onehot.shape, 0)
    onehot[...] = jnp.where(rows_of == served[...], 1.0, 0.0).astype(BF16)
    loads[1].wait()
    zout[...] = to_slabs(dot_tn(onehot[...], table[...]))

    pl.semaphore_wait(barrier, n_emb + n_bal + n_rep - 3)

    stride = 27 if n_emb % 3 else 1

    def exchange(src, dst, send, recv):
        own = pl.ds(pl.multiple_of(e * slab, slab), slab)

        @pl.loop(1, n_emb, unroll=9 if n_emb % 9 == 1 else 1)
        def _(k):
            to = lax.rem(e + stride * k, n_emb)
            pltpu.make_async_remote_copy(
                src_ref=src.at[pl.ds(pl.multiple_of(to * slab, slab), slab)],
                dst_ref=dst.at[own],
                send_sem=send,
                recv_sem=recv,
                device_id={"emb": to},
                device_id_type=MESH,
            ).start()

        dst[own, :] = src[own, :]
        many = pl.ds(0, (n_emb - 1) * slab)
        return pltpu.make_async_remote_copy(
            src_ref=src.at[many],
            dst_ref=dst.at[many],
            send_sem=send,
            recv_sem=recv,
            device_id={"emb": lax.rem(e + 1, n_emb)},
            device_id_type=MESH,
        )

    first = exchange(zout, zin, a1_send, a1_recv)

    loads[2].wait()
    slot_of = lax.broadcasted_iota(jnp.int32, look.shape, 0)
    hit = (slot_of == lookup[0:1, :]) | (slot_of == lookup[1:2, :])
    look[...] = jnp.where(hit, 1.0, 0.0).astype(BF16)

    my_user = users_ref[0, b]
    count = jnp.int32(0)
    for k in range(n_bal):
        count = count + jnp.where(users_ref[0, k] == my_user, 1, 0)
    inv_len = jnp.float32(0.0)
    for k in range(1, n_bal + 1):
        inv_len = jnp.where(count == k, jnp.float32(1.0 / (k * tok)), inv_len)

    for load in loads[3:]:
        load.wait()
    d_mixed[...] = dot_nt(grad[...], w_out[...])

    first.wait_recv()
    ev = dot_tn(look[...], from_slabs(zin[...]))
    events[...] = ev
    centered = ev - row_mean(ev)
    inv = lax.rsqrt(row_mean(centered * centered) + EPS)
    inv_in[...] = jnp.broadcast_to(inv, inv_in.shape)
    normed[...] = centered * inv
    nrm[0] = normed[...].astype(BF16)

    rows = tok // 4
    steps = n_bal // 2
    right = lax.rem(b + 1, n_bal)
    left = lax.rem(b + n_bal - 1, n_bal)

    def hop(buf, send, recv, way, step, c):
        if way == 0:
            src, dst, to = lax.rem(n_bal - step, n_bal), n_bal - 1 - step, right
        else:
            src, dst, to = step, step + 1, left
        piece = pl.ds(pl.multiple_of(c * rows, rows), rows)
        return pltpu.make_async_remote_copy(
            src_ref=buf.at[src, piece],
            dst_ref=buf.at[dst, piece],
            send_sem=send.at[way, step, c],
            recv_sem=recv.at[way, step, c],
            device_id={"bal": to},
            device_id_type=MESH,
        )

    def last_step(way, c):
        return jnp.where(lax.div(c, 2) == way, steps - 1, steps - 2)

    def used(causal, way, step, origin):
        if not causal:
            return step >= 0
        return origin >= steps if way == 0 else origin > step

    def sent(causal, way, step, c):
        origin = lax.rem(b + (n_bal - step if way == 0 else step), n_bal)
        return (step <= last_step(way, c)) & used(causal, way, step, origin)

    def received(causal, way, step, c):
        origin = lax.rem(b + (n_bal - 1 - step if way == 0 else step + 1), n_bal)
        return (step <= last_step(way, c)) & used(causal, way, step, origin)

    def ring_start(buf, send, recv, causal):
        @pl.loop(0, 4)
        def _(c):
            for way in range(2):
                @pl.when(sent(causal, way, 0, c))
                def _():
                    hop(buf, send, recv, way, 0, c).start()

    def ring_rest(buf, send, recv, causal, own_head, on_block):
        @pl.loop(0, steps + 1)
        def _(step):
            @pl.loop(0, 4)
            def _(c):
                for way in range(2):
                    @pl.when(received(causal, way, step, c))
                    def _():
                        hop(buf, send, recv, way, step, c).wait_recv()

                    @pl.when(sent(causal, way, step + 1, c))
                    def _():
                        hop(buf, send, recv, way, step + 1, c).start()

                @pl.when(step == 0)
                def _():
                    own_head(c)

                @pl.when((step > 0) & ((c == 1) | ((c == 3) & (step < steps))))
                def _():
                    on_block(jnp.where(c == 1, n_bal - step, step))

    def ring_drain(buf, send, recv, causal):
        @pl.loop(0, steps)
        def _(step):
            @pl.loop(0, 4)
            def _(c):
                for way in range(2):
                    @pl.when(sent(causal, way, step, c))
                    def _():
                        hop(buf, send, recv, way, step, c).wait_send()

    v_at, q_at, k_at = width, 2 * width, 3 * width

    def head(h, base=0):
        if isinstance(h, int):
            return slice(base + h * hd, base + (h + 1) * hd)
        return pl.ds(pl.multiple_of(base + h * hd, hd), hd)

    def project(*columns):
        for base in columns:
            cols = slice(base, base + width)
            a, s = silu_and_slope(dot(nrm[0], w_in[:, cols]))
            act[:, cols] = a.astype(BF16)
            slope[:, cols] = s

    def own_pair(h):
        tri_row = lax.broadcasted_iota(jnp.int32, (tok, tok), 0)
        tri_col = lax.broadcasted_iota(jnp.int32, (tok, tok), 1)
        q, k, v = act[:, head(h, q_at)], act[:, head(h, k_at)], act[:, head(h, v_at)]
        y, g = silu_and_slope(dot_nt(q, k) * inv_root)
        keep = tri_row >= tri_col
        att[:, head(h)] = dot(jnp.where(keep, y * inv_len, 0.0).astype(BF16), v)
        gq[0, h] = jnp.where(keep, g * inv_len, 0.0)
        y, g = silu_and_slope(dot_nt(k, q) * inv_root)
        keep = tri_row <= tri_col
        wt[0, h] = jnp.where(keep, y * inv_len, 0.0).astype(BF16)
        gt[0, h] = jnp.where(keep, g * inv_len, 0.0)

    ring_start(nrm, x1_send, x1_recv, False)
    project(q_at, k_at, v_at, 0)

    def seen(j):
        return jnp.where(users_ref[0, j] == my_user, inv_len, jnp.float32(0.0))

    def forward_block(r):
        j = lax.rem(b + r, n_bal)
        f = seen(j)

        @pl.when(j < b)
        def _():
            x = nrm[r]
            kv[r, :, :width] = silu(dot(x, w_in[:, v_at : v_at + width])).astype(BF16)
            kv[r, :, width:] = silu(dot(x, w_in[:, k_at : k_at + width])).astype(BF16)
            for h in range(HEADS):
                k = kv[r, :, head(h, width)]
                y, g = silu_and_slope(dot_nt(act[:, head(h, q_at)], k) * inv_root)
                gq[r, h] = g * f
                att[:, head(h)] += dot((y * f).astype(BF16), kv[r, :, head(h)])

        @pl.when(j > b)
        def _():
            qall[r] = silu(dot(nrm[r], w_in[:, q_at : q_at + width])).astype(BF16)
            for h in range(HEADS):
                y, g = silu_and_slope(
                    dot_nt(act[:, head(h, k_at)], qall[r, :, head(h)]) * inv_root
                )
                gt[r, h] = g * f
                wt[r, h] = (y * f).astype(BF16)

    ring_rest(nrm, x1_send, x1_recv, False, own_pair, forward_block)

    at = att[...]
    centered = at - row_mean(at)
    inv_att = lax.rsqrt(row_mean(centered * centered) + EPS)
    na = centered * inv_att
    normed_att[...] = na
    d_gated = d_mixed[...] * act[:, :width].astype(F32)
    d_att = (
        (d_gated - row_mean(d_gated) - na * row_mean(d_gated * na)) * inv_att
    ).astype(BF16)
    datt[0] = d_att

    def own_pair_back(h):
        q, k, v = act[:, head(h, q_at)], act[:, head(h, k_at)], act[:, head(h, v_at)]
        d = datt[0, :, head(h)]
        ds = (dot_nt(d, v) * gq[0, h]).astype(BF16)
        dq[:, head(h)] = dot(ds, k)
        dv[:, head(h)] = dot(wt[0, h], d)
        dst = (dot_nt(v, d) * gt[0, h]).astype(BF16)
        dk[:, head(h)] = dot(dst, q)

    def own_layer():
        mixed = (normed_att[...] * act[:, :width].astype(F32)).astype(BF16)
        layer_ref[...] = (events[...] + dot(mixed, w_out[...])).astype(BF16)

    def own_gate():
        d_pre = (d_mixed[...] * normed_att[...] * slope[:, :width]).astype(BF16)
        dn[...] = dot_nt(d_pre, w_in[:, :width])

    ring_start(datt, x2_send, x2_recv, True)
    own_layer()
    own_gate()

    def backward_block(r):
        j = lax.rem(b + r, n_bal)

        @pl.when(j < b)
        def _():
            for h in range(HEADS):
                ds = (dot_nt(datt[0, :, head(h)], kv[r, :, head(h)]) * gq[r, h]).astype(BF16)
                dq[:, head(h)] += dot(ds, kv[r, :, head(h, width)])

        @pl.when(j > b)
        def _():
            for h in range(HEADS):
                d = datt[r, :, head(h)]
                dv[:, head(h)] += dot(wt[r, h], d)
                dst = (dot_nt(act[:, head(h, v_at)], d) * gt[r, h]).astype(BF16)
                dk[:, head(h)] += dot(dst, qall[r, :, head(h)])

    ring_rest(datt, x2_send, x2_recv, True, own_pair_back, backward_block)

    d_normed = dn[...]
    for base, acc, scale in ((v_at, dv, 1.0), (q_at, dq, inv_root), (k_at, dk, inv_root)):
        d_pre = (acc[...] * scale * slope[:, base : base + width]).astype(BF16)
        d_normed = d_normed + dot_nt(d_pre, w_in[:, base : base + width])
    nr = normed[...]
    d_events = (
        grad[...].astype(F32)
        + (d_normed - row_mean(d_normed) - nr * row_mean(d_normed * nr)) * inv_in[:, 0:1]
    ).astype(BF16)

    zback[...] = to_slabs(dot(look[...], d_events))
    second = exchange(zback, zret, a2_send, a2_recv)
    first.wait_send()
    ring_drain(nrm, x1_send, x1_recv, False)
    ring_drain(datt, x2_send, x2_recv, True)
    second.wait_recv()

    ours = pl.ds(pl.multiple_of(rep * share, share), share)
    theirs = pl.ds(pl.multiple_of((n_rep - 1 - rep) * share, share), share)
    own_part = pl.ds(pl.multiple_of(b * part, part), part)
    mine_at = pl.ds(pl.multiple_of(rep * share + b * part, part), part)
    others = pl.ds(0, (n_bal - 1) * part)
    other_core = {"rep": n_rep - 1 - rep}

    def remote(src, dst, send, recv, where):
        return pltpu.make_async_remote_copy(
            src_ref=src, dst_ref=dst, send_sem=send, recv_sem=recv,
            device_id=where, device_id_type=MESH,
        )

    both = range(2)
    swaps = [
        remote(gsend.at[c, theirs], cbuf.at[c], core_send.at[c], core_recv.at[c], other_core)
        for c in both
    ]
    fans = [
        remote(agbuf.at[c, ours], agbuf.at[c, ours], fan_send.at[c], fan_recv.at[c], other_core)
        for c in both
    ]
    reduced = [
        remote(
            hsend.at[c, others], rsbuf.at[c, others], rs_send.at[c], rs_recv.at[c],
            {"bal": right},
        )
        for c in both
    ]
    gathered = [
        remote(
            agbuf.at[c, others], agbuf.at[c, others], ag_send.at[c], ag_recv.at[c],
            {"bal": right},
        )
        for c in both
    ]
    apart = zret[...].astype(F32).reshape(n_emb, 2, cap, half)
    for c in both:
        back = apart[:, c].reshape(slots, half).astype(BF16)
        gsend[c] = dot(onehot[...], back).astype(BF16)
        if n_rep == 2:
            swaps[c].start()

    for c in both:
        if n_rep == 2:
            swaps[c].wait_recv()
            hsend[c] = (gsend[c, ours, :].astype(F32) + cbuf[c].astype(F32)).astype(BF16)
        else:
            hsend[c] = gsend[c]

        @pl.loop(1, n_bal, unroll=n_bal - 1)
        def _(k):
            to = lax.rem(b + k, n_bal)
            remote(
                hsend.at[c, pl.ds(pl.multiple_of(to * part, part), part)],
                rsbuf.at[c, own_part], rs_send.at[c], rs_recv.at[c], {"bal": to},
            ).start()

        rsbuf[c, own_part, :] = hsend[c, own_part, :]

    second.wait_send()
    for c in both:
        reduced[c].wait_recv()
        total = rsbuf[c, 0:part, :].astype(F32)
        for k in range(1, n_bal):
            total = total + rsbuf[c, k * part : (k + 1) * part, :].astype(F32)
        agbuf[c, mine_at, :] = total.astype(BF16)

        @pl.loop(1, n_bal, unroll=n_bal - 1)
        def _(k):
            remote(
                agbuf.at[c, mine_at], agbuf.at[c, mine_at], ag_send.at[c], ag_recv.at[c],
                {"bal": lax.rem(b + k, n_bal)},
            ).start()

    for c in both:
        gathered[c].wait_recv()
        if n_rep == 2:
            fans[c].start()
    for c in both:
        if n_rep == 2:
            fans[c].wait_recv()
        tgrad_ref[:, c * half : (c + 1) * half] = agbuf[c]
    for c in both:
        reduced[c].wait_send()
        gathered[c].wait_send()
        if n_rep == 2:
            swaps[c].wait_send()
            fans[c].wait_send()


def per_device(table, served_rows, w_in, w_out, lookup_slots, block_users, out_grad):
    n_emb, n_bal, n_rep = (lax.axis_size(a) for a in ("emb", "bal", "rep"))
    trows, width = table.shape
    tok = lookup_slots.shape[1]
    half = width // 2
    steps = n_bal // 2
    slots = 2 * served_rows.shape[-1]
    hd = width // HEADS
    vmem = pl.BlockSpec(memory_space=pltpu.VMEM)
    hbm = pl.BlockSpec(memory_space=pltpu.HBM)
    dma = pltpu.SemaphoreType.DMA
    share = trows // n_rep
    layer_out, table_grad = pl.pallas_call(
        functools.partial(layer_kernel, (n_emb, n_bal, n_rep)),
        out_shape=(
            pltpu.VMEM((tok, width), BF16),
            pltpu.VMEM((trows, width), BF16),
        ),
        in_specs=[hbm, hbm, hbm, pl.BlockSpec(memory_space=pltpu.SMEM), hbm, hbm, hbm],
        out_specs=(vmem, vmem),
        scratch_shapes=[
            pltpu.VMEM((trows, width), BF16),
            pltpu.VMEM((1, slots // 2), jnp.int32),
            pltpu.VMEM((2, tok), jnp.int32),
            pltpu.VMEM((width, 4 * width), BF16),
            pltpu.VMEM((width, width), BF16),
            pltpu.VMEM((tok, width), BF16),
            pltpu.VMEM((slots, half), BF16),
            pltpu.VMEM((slots, half), BF16),
            pltpu.VMEM((slots, half), BF16),
            pltpu.VMEM((slots, half), BF16),
            pltpu.VMEM((trows, slots // 2), BF16),
            pltpu.VMEM((slots // 2, tok), BF16),
            pltpu.VMEM((tok, width), F32),
            pltpu.VMEM((tok, width), F32),
            pltpu.VMEM((tok, 128), F32),
            pltpu.VMEM((tok, 4 * width), BF16),
            pltpu.VMEM((tok, 4 * width), F32),
            pltpu.VMEM((n_bal, tok, width), BF16),
            pltpu.VMEM((n_bal, tok, width), BF16),
            pltpu.VMEM((n_bal, tok, 2 * width), BF16),
            pltpu.VMEM((n_bal, tok, width), BF16),
            pltpu.VMEM((n_bal, HEADS, tok, tok), BF16),
            pltpu.VMEM((n_bal, HEADS, tok, tok), F32),
            pltpu.VMEM((n_bal, HEADS, tok, tok), F32),
            pltpu.VMEM((tok, width), F32),
            pltpu.VMEM((tok, width), F32),
            pltpu.VMEM((tok, width), F32),
            pltpu.VMEM((tok, width), F32),
            pltpu.VMEM((tok, width), F32),
            pltpu.VMEM((tok, width), F32),
            pltpu.VMEM((tok, width), F32),
            pltpu.VMEM((2, trows, half), BF16),
            pltpu.VMEM((2, share, half), BF16),
            pltpu.VMEM((2, share, half), BF16),
            pltpu.VMEM((2, share, half), BF16),
            pltpu.VMEM((2, trows, half), BF16),
            dma((6,)),
            dma, dma,
            dma((2, steps, 4)), dma((2, steps, 4)),
            dma((2, steps, 4)), dma((2, steps, 4)),
            dma, dma,
            dma((2,)), dma((2,)), dma((2,)), dma((2,)),
            dma((2,)), dma((2,)), dma((2,)), dma((2,)),
        ],
        compiler_params=pltpu.CompilerParams(
            collective_id=0, has_side_effects=True, vmem_limit_bytes=56 * 1024 * 1024
        ),
    )(
        table, served_rows.reshape(1, -1), lookup_slots[0].T, block_users, w_in, w_out, out_grad[0],
    )
    return layer_out[None], table_grad.astype(F32)


def solution(mesh):
    placed = (
        P("emb", None),
        P("emb", "bal", "rep", None),
        P(),
        P(),
        P(("emb", "rep"), "bal", None),
        P(("emb", "rep"), None),
        P(("emb", "rep"), "bal", None),
    )
    return jax.shard_map(
        per_device,
        mesh=mesh,
        in_specs=placed,
        out_specs=(P(("emb", "rep"), "bal", None), P("emb", None)),
        check_vma=False,
    )
```
